32 devices in a mesh: dp: 4 (over y, x), seq: 8 (over z, core).
Axes of the slice: x: 2, y: 2, z: 4, core: 2. Of those that a mesh axis runs over, the one named last changes fastest.
Arguments:
- long_frames: bfloat16 [8, 640, 1024], P('dp', 'seq'), may hold values from -6 to 6
- short_frames: bfloat16 [8, 512, 1024], P('dp', 'seq'), may hold values from -6 to 6
- long_text: bfloat16 [8, 64, 768], P('dp'), may hold values from -6 to 6
- short_text: bfloat16 [8, 64, 768], P('dp'), may hold values from -6 to 6
- long_lengths: int32 [8], P('dp'), may hold values from 320 to 640, as said below
- short_lengths: int32 [8], P('dp'), may hold values from 256 to 512, as said below
- text_lengths: int32 [2, 8], P(None, 'dp'), may hold values from 32 to 64, as said below
- qkv_weight: bfloat16 [1024, 3072], P('seq'), may hold values from -0.1875 to 0.1875
- self_out: bfloat16 [1024, 1024], P('seq'), may hold values from -1.5 to 1.5
- cross_query: bfloat16 [1024, 1024], P('seq'), may hold values from -0.1875 to 0.1875
- cross_keyval: bfloat16 [1024, 2048], P('seq'), may hold values from -0.1875 to 0.1875
- cross_out: bfloat16 [1024, 1024], P('seq'), may hold values from -0.75 to 0.75
- text_proj: bfloat16 [768, 1024], P('seq'), may hold values from -0.21875 to 0.21875
- text_bias: bfloat16 [1024], P('seq'), may hold values from -3 to 3
- feed_in: bfloat16 [1024, 4096], P('seq'), may hold values from -0.1875 to 0.1875
- feed_out: bfloat16 [4096, 1024], P('seq'), may hold values from -0.09375 to 0.09375
- norm_gains: bfloat16 [3, 1024], P(None, 'seq'), may hold values from 0.5 to 1.5
- norm_shifts: bfloat16 [3, 1024], P(None, 'seq'), may hold values from -2 to 2
- long_cot: bfloat16 [8, 640, 1024], P('dp', 'seq'), may hold values from -6 to 6
- short_cot: bfloat16 [8, 512, 1024], P('dp', 'seq'), may hold values from -6 to 6
Outputs:
- long_output: bfloat16 [8, 640, 1024], P('dp', 'seq')
- short_output: bfloat16 [8, 512, 1024], P('dp', 'seq')
- long_input_grad: float32 [8, 640, 1024], P('dp', 'seq')
- short_input_grad: float32 [8, 512, 1024], P('dp', 'seq')
- long_text_grad: float32 [8, 64, 768], P('dp', 'seq')
- short_text_grad: float32 [8, 64, 768], P('dp', 'seq')
- qkv_grad: float32 [1024, 3072], P('seq')
- self_out_grad: float32 [1024, 1024], P('seq')
- cross_query_grad: float32 [1024, 1024], P('seq')
- cross_keyval_grad: float32 [1024, 2048], P('seq')
- cross_out_grad: float32 [1024, 1024], P('seq')
- text_proj_grad: float32 [768, 1024], P('seq')
- text_bias_grad: float32 [1024], P('seq')
- feed_in_grad: float32 [1024, 4096], P('seq')
- feed_out_grad: float32 [4096, 1024], P('seq')
- gains_grad: float32 [3, 1024], P(None, 'seq')
- shifts_grad: float32 [3, 1024], P(None, 'seq')
The draws below stay inside these ranges and needn't reach their ends.
Inputs may be any that keep to these rules, and one draw needn't show every extreme that they name: `long_lengths`: frames of a long item at or past its length are padding that no frame attends to; in every draw some long item has all 640. `short_lengths`: frames of a short item at or past its length are padding that no frame attends to; in every draw some short item has all 512. `text_lengths`: an item's frames attend to its first that many text states; in each row some item has all 64.
All inputs are finite; a program needn't handle non-finite values.
Results may differ from the reference program's by a relative error of at most 0.025.
Values may be sent and summed in bfloat16 or wider, within the bound.
No kernel may reach another device: no remote copies, remote signals or barrier semaphores. Data moves between devices by JAX's collectives and lax.ppermute only.
A program may use at most 256 MiB of HBM per device.

```python
import jax
import jax.numpy as jnp
from jax import lax

D = 1024
HEADS = 16
FF = 4096
ENC = 768
TEXT = 64
ITEMS = 8
LEN_LONG = 640
LEN_SHORT = 512


def full_lengths(key, count, longest):
    lengths = jax.random.randint(key, (count,), longest // 2, longest + 1)
    chosen = jax.random.randint(jax.random.fold_in(key, 7), (), 0, count)
    return jnp.where(jnp.arange(count) == chosen, longest, lengths).astype(jnp.int32)


def draw_long_lengths(key, part):
    key = jax.random.fold_in(key, 1)
    return full_lengths(key, ITEMS, LEN_LONG)


def draw_short_lengths(key, part):
    key = jax.random.fold_in(key, 2)
    return full_lengths(key, ITEMS, LEN_SHORT)


def draw_text_lengths(key, part):
    key = jax.random.fold_in(key, 3)
    first = full_lengths(jax.random.fold_in(key, 4), ITEMS, TEXT)
    second = full_lengths(jax.random.fold_in(key, 5), ITEMS, TEXT)
    return jnp.stack([first, second]).astype(jnp.int32)


def shard_levels(own_key, shape, split, least, high):
    def one(dim, shards_of):
        steps = jax.random.uniform(jax.random.fold_in(jax.random.fold_in(own_key, 6), dim), (shards_of,), jnp.float32, least / len(split), high / len(split))
        return jnp.repeat(jnp.exp(steps), shape[dim] // shards_of).reshape((-1,) + (1,) * (len(shape) - dim - 1))

    gain = one(*split[0])
    for cut in split[1:]:
        gain = gain * one(*cut)
    return gain


def scatter_about(key, shape, scale, bound, pieces=(), dtype=jnp.bfloat16):
    values = jax.random.normal(key, shape, jnp.float32) * scale
    if len(pieces) > 0:
        values = shard_levels(key, shape, pieces, -0.22, 0.18) * values
    return jnp.clip(values, min=-bound, max=bound).astype(dtype)


def setup_inputs(seed: int = 0) -> dict:
    splits = jax.random.split(jax.random.key(seed), 21)
    long_frames = scatter_about(splits[0], (ITEMS, LEN_LONG, D), 1.0, 6.0, ((0, 4), (1, 8)))
    short_frames = scatter_about(splits[1], (ITEMS, LEN_SHORT, D), 1.0, 6.0, ((0, 4), (1, 8)))
    long_text = scatter_about(splits[2], (ITEMS, TEXT, ENC), 1.0, 6.0, ((0, 4),))
    short_text = scatter_about(splits[3], (ITEMS, TEXT, ENC), 1.0, 6.0, ((0, 4),))
    long_lengths = draw_long_lengths(jax.random.fold_in(splits[20], 71), 0)
    short_lengths = draw_short_lengths(jax.random.fold_in(splits[20], 71), 0)
    text_lengths = draw_text_lengths(jax.random.fold_in(splits[20], 71), 0)
    qkv_weight = scatter_about(splits[7], (D, 3 * D), D ** -0.5, 0.1875, ((0, 8),))
    self_out = scatter_about(splits[8], (D, D), (D // 64) ** -0.5, 1.5, ((0, 8),))
    cross_query = scatter_about(splits[9], (D, D), D ** -0.5, 0.1875, ((0, 8),))
    cross_keyval = scatter_about(splits[10], (D, 2 * D), D ** -0.5, 0.1875, ((0, 8),))
    cross_out = scatter_about(splits[11], (D, D), (D // 16) ** -0.5, 0.75, ((0, 8),))
    text_proj = scatter_about(splits[12], (ENC, D), ENC ** -0.5, 0.21875, ((0, 8),))
    text_bias = scatter_about(splits[13], (D,), 0.5, 3.0, ((0, 8),))
    feed_in = scatter_about(splits[14], (D, FF), D ** -0.5, 0.1875, ((0, 8),))
    feed_out = scatter_about(splits[15], (FF, D), FF ** -0.5, 0.09375, ((0, 8),))
    norm_gains = jnp.clip(0.5 + 1.0 * jax.random.uniform(splits[16], (3, D), jnp.float32) ** shard_levels(splits[16], (3, D), ((1, 8),), -0.2, 0.2), 0.5, 1.5).astype(jnp.bfloat16)
    norm_shifts = scatter_about(splits[17], (3, D), 0.3, 2.0, ((1, 8),))
    long_cot = scatter_about(splits[18], (ITEMS, LEN_LONG, D), 1.0, 6.0, ((0, 4), (1, 8)))
    short_cot = scatter_about(splits[19], (ITEMS, LEN_SHORT, D), 1.0, 6.0, ((0, 4), (1, 8)))
    return dict(long_frames=long_frames, short_frames=short_frames, long_text=long_text, short_text=short_text, long_lengths=long_lengths, short_lengths=short_lengths, text_lengths=text_lengths, qkv_weight=qkv_weight, self_out=self_out, cross_query=cross_query, cross_keyval=cross_keyval, cross_out=cross_out, text_proj=text_proj, text_bias=text_bias, feed_in=feed_in, feed_out=feed_out, norm_gains=norm_gains, norm_shifts=norm_shifts, long_cot=long_cot, short_cot=short_cot)


@jax.custom_vjp
def low(v):
    return lax.optimization_barrier(v.astype(jnp.bfloat16)).astype(jnp.float32)

@jax.custom_vjp
def low_back(v):
    return v

def low_keep(v):
    return (low(v), None)

def low_pass(kept, grad):
    return (grad,)

def back_keep(v):
    return (v, None)

def back_low(kept, grad):
    return (low(grad),)
low.defvjp(low_keep, low_pass)
low_back.defvjp(back_keep, back_low)
highest = lax.Precision.HIGHEST
masked_value = -1e+30
norm_eps = 1e-05

def layer_norm(values, gain_row, bias_row):
    average = lax.optimization_barrier(jnp.mean(values, -1, keepdims=True))
    centred = values - average
    spread = lax.optimization_barrier(jnp.mean(centred * centred, -1, keepdims=True))
    return centred * lax.rsqrt(spread + norm_eps) * gain_row + bias_row

def matmul(left, right):
    return jnp.matmul(left, right, precision=highest)

def split_heads(matrix):
    return matrix.reshape(matrix.shape[0], HEADS, -1).transpose(1, 0, 2)

def merge_heads(tensor):
    return tensor.transpose(1, 0, 2).reshape(tensor.shape[1], -1)

def attend(query, keys, values, mask, score_scale):
    scores = low_back(jnp.einsum('hqd,hkd->hqk', query, keys, precision=highest) * score_scale)
    scores = jnp.where(mask, scores, masked_value)
    weights = jax.nn.softmax(scores, axis=-1)
    return jnp.einsum('hqk,hkd->hqd', low(weights), values, precision=highest)

def layer(frames, words, length, text_length, params):
    w_qkv, w_self, w_query, w_keyval, w_cross, w_text, b_text, w_in, w_out, gains, shifts = params
    full = frames.shape[0]
    score_scale = (D // HEADS) ** (-0.5)
    normed = low(layer_norm(frames, gains[0], shifts[0]))
    packed = low_back(low(matmul(normed, w_qkv)))
    places = jnp.arange(full)
    self_mask = (places[:, None] >= places[None, :]) & (places[None, :] < length)
    mixed = attend(split_heads(packed[:, :D]), split_heads(packed[:, D:2 * D]), split_heads(packed[:, 2 * D:]), self_mask, score_scale)
    mixed = low_back(low(merge_heads(mixed)))
    after_self = frames + low_back(matmul(mixed, w_self))
    normed_cross = low(layer_norm(after_self, gains[1], shifts[1]))
    cross_q = low_back(low(matmul(normed_cross, w_query)))
    encoded = low_back(low(matmul(words, w_text) + b_text))
    keyval = low_back(low(matmul(encoded, w_keyval)))
    text_mask = (jnp.arange(TEXT) < text_length)[None, :]
    cross_mixed = attend(split_heads(cross_q), split_heads(keyval[:, :D]), split_heads(keyval[:, D:]), text_mask, score_scale)
    cross_mixed = low_back(low(merge_heads(cross_mixed)))
    after_cross = after_self + low_back(matmul(cross_mixed, w_cross))
    normed_feed = low(layer_norm(after_cross, gains[2], shifts[2]))
    pre_act = low_back(matmul(normed_feed, w_in))
    hidden = low(jax.nn.gelu(pre_act, approximate=False))
    return after_cross + low_back(matmul(hidden, w_out))

def bucket(frames, texts, lengths, text_lens, cots, params):

    def step(totals, item):
        frame, words, length, text_length, cotangent = item

        def forward(frame_v, text_v, *weights):
            return layer(frame_v, text_v, length, text_length, weights)
        output, pullback = jax.vjp(forward, frame.astype(jnp.float32), words.astype(jnp.float32), *params)
        grads = pullback(cotangent.astype(jnp.float32))
        totals = tuple((total + grad for total, grad in zip(totals, grads[2:])))
        return (totals, (output.astype(jnp.bfloat16), grads[0], grads[1]))
    zeros = tuple((jnp.zeros_like(weight) for weight in params))
    return lax.scan(step, zeros, (frames, texts, lengths, text_lens, cots))

def reference(long_frames, short_frames, long_text, short_text, long_lengths, short_lengths, text_lengths, qkv_weight, self_out, cross_query, cross_keyval, cross_out, text_proj, text_bias, feed_in, feed_out, norm_gains, norm_shifts, long_cot, short_cot):
    params = tuple((weight.astype(jnp.float32) for weight in (qkv_weight, self_out, cross_query, cross_keyval, cross_out, text_proj, text_bias, feed_in, feed_out, norm_gains, norm_shifts)))
    long_totals, long_parts = bucket(long_frames, long_text, long_lengths, text_lengths[0], long_cot, params)
    short_totals, short_parts = bucket(short_frames, short_text, short_lengths, text_lengths[1], short_cot, params)
    grads = [first + second for first, second in zip(long_totals, short_totals)]
    return (long_parts[0], short_parts[0], long_parts[1], short_parts[1], long_parts[2], short_parts[2], grads[0], grads[1], grads[2], grads[3], grads[4], grads[5], grads[6], grads[7], grads[8], grads[9], grads[10])
```

```python
from functools import partial

import jax
import jax.numpy as jnp
from jax import lax
from jax.experimental import pallas as pl
from jax.experimental.pallas import tpu as pltpu
from jax.sharding import PartitionSpec as P

D = 1024
HEADS = 16
ENC = 768
TEXT = 64


masked_value = -1e30
norm_eps = 1e-05


def layer_norm(values, gain_row, bias_row):
    average = jnp.mean(values, -1, keepdims=True)
    centred = values - average
    spread = jnp.mean(centred * centred, -1, keepdims=True)
    return centred * lax.rsqrt(spread + norm_eps) * gain_row + bias_row


def norm_back(values, gain_row, bias_row, incoming):
    _, pullback = jax.vjp(layer_norm, values, gain_row, bias_row)
    return pullback(incoming)


def product(left, right):
    return jnp.dot(left, right, preferred_element_type=jnp.float32)


def product_t(left, right):
    return lax.dot_general(
        left, right, (((left.ndim - 1,), (1,)), ((), ())), preferred_element_type=jnp.float32
    )


def weight_grad(left, right):
    return lax.dot_general(
        left, right, (((0,), (0,)), ((), ())), preferred_element_type=jnp.float32
    )


def head_view(packed, head_dim):
    return packed.reshape(packed.shape[0], packed.shape[1], -1, head_dim)


def flatten_heads(tensor):
    return tensor.reshape(tensor.shape[0], tensor.shape[1], -1).astype(jnp.bfloat16)


def softmax_weights(query, keys, mask, score_scale):
    scores = (
        jnp.einsum("iqhd,ikhd->ihqk", query, keys, preferred_element_type=jnp.float32) * score_scale
    )
    scores = jnp.where(mask, scores, masked_value)
    row_max = jnp.max(scores, -1, keepdims=True)
    raised = jnp.exp(scores - row_max)
    return raised / jnp.sum(raised, -1, keepdims=True)


def attend_forward(query, keys, values, mask, score_scale):
    weights = softmax_weights(query, keys, mask, score_scale).astype(jnp.bfloat16)
    mixed = jnp.einsum("ihqk,ikhd->iqhd", weights, values, preferred_element_type=jnp.float32)
    return flatten_heads(mixed)


def attend_backward(query, keys, values, mask, score_scale, grad_out):
    probs = softmax_weights(query, keys, mask, score_scale)
    grad_values = jnp.einsum(
        "ihqk,iqhd->ikhd", probs.astype(jnp.bfloat16), grad_out, preferred_element_type=jnp.float32
    )
    grad_probs = jnp.einsum("iqhd,ikhd->ihqk", grad_out, values, preferred_element_type=jnp.float32)
    centre = jnp.sum(probs * grad_probs, -1, keepdims=True)
    grad_scores = (probs * (grad_probs - centre)).astype(jnp.bfloat16)
    grad_query = (
        jnp.einsum("ihqk,ikhd->iqhd", grad_scores, keys, preferred_element_type=jnp.float32)
        * score_scale
    )
    grad_keys = (
        jnp.einsum("ihqk,iqhd->ikhd", grad_scores, query, preferred_element_type=jnp.float32)
        * score_scale
    )
    return (flatten_heads(grad_query), flatten_heads(grad_keys), flatten_heads(grad_values))


def on_device(
    long_frames,
    short_frames,
    long_text,
    short_text,
    long_lengths,
    short_lengths,
    text_lengths,
    qkv_weight,
    self_out,
    cross_query,
    cross_keyval,
    cross_out,
    text_proj,
    text_bias,
    feed_in,
    feed_out,
    norm_gains,
    norm_shifts,
    long_cot,
    short_cot,
):
    w_qkv, w_self, w_query, w_keyval, w_cross, w_text, b_text, w_in, w_out, gains, shifts = (
        lax.all_gather(qkv_weight, "seq", axis=0, tiled=True),
        lax.all_gather(self_out, "seq", axis=0, tiled=True),
        lax.all_gather(cross_query, "seq", axis=0, tiled=True),
        lax.all_gather(cross_keyval, "seq", axis=0, tiled=True),
        lax.all_gather(cross_out, "seq", axis=0, tiled=True),
        lax.all_gather(text_proj, "seq", axis=0, tiled=True),
        lax.all_gather(text_bias, "seq", axis=0, tiled=True),
        lax.all_gather(feed_in, "seq", axis=0, tiled=True),
        lax.all_gather(feed_out, "seq", axis=0, tiled=True),
        lax.all_gather(norm_gains, "seq", axis=1, tiled=True),
        lax.all_gather(norm_shifts, "seq", axis=1, tiled=True),
    )
    seq_count = lax.axis_size("seq")
    seq_rank = lax.axis_index("seq")
    head_dim = D // HEADS
    head_width = D // seq_count
    score_scale = head_dim ** (-0.5)
    item_count, long_rows, _ = long_frames.shape
    short_rows = short_frames.shape[1]
    long_total = item_count * long_rows
    long_len = long_rows * seq_count
    short_len = short_rows * seq_count

    def to_items(joined):
        last_dim = joined.shape[-1]
        return (
            joined[:long_total].reshape(item_count, long_rows, last_dim),
            joined[long_total:].reshape(item_count, short_rows, last_dim),
        )

    def to_rows(long_part, short_part):
        return jnp.concatenate(
            [
                long_part.reshape(long_part.shape[0] * long_part.shape[1], -1),
                short_part.reshape(short_part.shape[0] * short_part.shape[1], -1),
            ],
            0,
        )

    def self_mask(lengths, full):
        places = jnp.arange(full)
        causal = places[:, None] >= places[None, :]
        return causal[None, None] & (places[None, None, None, :] < lengths[:, None, None, None])

    def text_mask(lengths):
        places = jnp.arange(TEXT)
        return (places[None, :] < lengths[:, None])[:, None, None, :]

    def split_three(packed):
        return (
            head_view(packed[:, :, 0], head_dim),
            head_view(packed[:, :, 1], head_dim),
            head_view(packed[:, :, 2], head_dim),
        )

    masks_self = (self_mask(long_lengths, long_len), self_mask(short_lengths, short_len))
    masks_text = (text_mask(text_lengths[0]), text_mask(text_lengths[1]))
    inputs = to_rows(long_frames, short_frames).astype(jnp.float32)
    normed_self = layer_norm(inputs, gains[0], shifts[0]).astype(jnp.bfloat16)

    def self_heads():
        packed = product(normed_self, w_qkv).astype(jnp.bfloat16)
        long_part, short_part = to_items(packed)
        long_part = long_part.reshape(item_count, long_rows, 3, D)
        short_part = short_part.reshape(item_count, short_rows, 3, D)
        return (
            lax.all_to_all(long_part, "seq", split_axis=3, concat_axis=1, tiled=True),
            lax.all_to_all(short_part, "seq", split_axis=3, concat_axis=1, tiled=True),
        )

    heads_pair = self_heads()
    long_mixed = attend_forward(*split_three(heads_pair[0]), masks_self[0], score_scale)
    short_mixed = attend_forward(*split_three(heads_pair[1]), masks_self[1], score_scale)
    long_back, short_back = (
        lax.all_to_all(long_mixed, "seq", split_axis=1, concat_axis=2, tiled=True),
        lax.all_to_all(short_mixed, "seq", split_axis=1, concat_axis=2, tiled=True),
    )
    self_rows = to_rows(long_back, short_back)
    after_self = inputs + product(self_rows, w_self)
    normed_cross = layer_norm(after_self, gains[1], shifts[1]).astype(jnp.bfloat16)
    long_query, short_query = to_items(product(normed_cross, w_query).astype(jnp.bfloat16))
    query_heads = (
        lax.all_to_all(long_query, "seq", split_axis=2, concat_axis=1, tiled=True),
        lax.all_to_all(short_query, "seq", split_axis=2, concat_axis=1, tiled=True),
    )
    key_cols = lax.dynamic_slice_in_dim(w_keyval, seq_rank * head_width, head_width, 1)
    value_cols = lax.dynamic_slice_in_dim(w_keyval, D + seq_rank * head_width, head_width, 1)
    texts = (long_text, short_text)
    encoded = tuple(((product(words, w_text) + b_text).astype(jnp.bfloat16) for words in texts))
    text_keys = tuple((product(enc_rows, key_cols).astype(jnp.bfloat16) for enc_rows in encoded))
    text_values = tuple(
        (product(enc_rows, value_cols).astype(jnp.bfloat16) for enc_rows in encoded)
    )
    cross_long = attend_forward(
        head_view(query_heads[0], head_dim),
        head_view(text_keys[0], head_dim),
        head_view(text_values[0], head_dim),
        masks_text[0],
        score_scale,
    )
    cross_short = attend_forward(
        head_view(query_heads[1], head_dim),
        head_view(text_keys[1], head_dim),
        head_view(text_values[1], head_dim),
        masks_text[1],
        score_scale,
    )
    cross_back_long, cross_back_short = (
        lax.all_to_all(cross_long, "seq", split_axis=1, concat_axis=2, tiled=True),
        lax.all_to_all(cross_short, "seq", split_axis=1, concat_axis=2, tiled=True),
    )
    cross_rows = to_rows(cross_back_long, cross_back_short)
    after_cross = after_self + product(cross_rows, w_cross)
    normed_feed = layer_norm(after_cross, gains[2], shifts[2]).astype(jnp.bfloat16)
    pre_act = product(normed_feed, w_in)
    hidden = jax.nn.gelu(pre_act, approximate=False).astype(jnp.bfloat16)
    result = after_cross + product(hidden, w_out)
    grad_rows = to_rows(long_cot, short_cot)
    feed_out_grad = weight_grad(hidden, grad_rows)
    _, gelu_pull = jax.vjp(partial(jax.nn.gelu, approximate=False), pre_act)
    grad_pre = gelu_pull(product_t(grad_rows, w_out))[0].astype(jnp.bfloat16)
    feed_in_grad = weight_grad(normed_feed, grad_pre)
    grad_cross_in, gain_two, shift_two = norm_back(
        after_cross, gains[2], shifts[2], product_t(grad_pre, w_in)
    )
    grad_after_cross = grad_rows.astype(jnp.float32) + grad_cross_in
    cross_branch = grad_after_cross.astype(jnp.bfloat16)
    cross_out_grad = weight_grad(cross_rows, cross_branch)
    long_dco, short_dco = to_items(product_t(cross_branch, w_cross).astype(jnp.bfloat16))
    grad_heads = (
        lax.all_to_all(long_dco, "seq", split_axis=2, concat_axis=1, tiled=True),
        lax.all_to_all(short_dco, "seq", split_axis=2, concat_axis=1, tiled=True),
    )
    cross_parts = tuple(
        (
            attend_backward(
                head_view(query_heads[bucket], head_dim),
                head_view(text_keys[bucket], head_dim),
                head_view(text_values[bucket], head_dim),
                masks_text[bucket],
                score_scale,
                head_view(grad_heads[bucket], head_dim),
            )
            for bucket in range(2)
        )
    )
    long_dq, short_dq = (
        lax.all_to_all(cross_parts[0][0], "seq", split_axis=1, concat_axis=2, tiled=True),
        lax.all_to_all(cross_parts[1][0], "seq", split_axis=1, concat_axis=2, tiled=True),
    )
    query_rows = to_rows(long_dq, short_dq)
    cross_query_grad = weight_grad(normed_cross, query_rows)
    grad_self_in, gain_one, shift_one = norm_back(
        after_self, gains[1], shifts[1], product_t(query_rows, w_query)
    )
    grad_after_self = grad_after_cross + grad_self_in
    key_grad = jnp.zeros((D, head_width), jnp.float32)
    value_grad = jnp.zeros((D, head_width), jnp.float32)
    for bucket in range(2):
        key_grad = key_grad + jnp.einsum(
            "itd,itw->dw",
            encoded[bucket],
            cross_parts[bucket][1],
            preferred_element_type=jnp.float32,
        )
        value_grad = value_grad + jnp.einsum(
            "itd,itw->dw",
            encoded[bucket],
            cross_parts[bucket][2],
            preferred_element_type=jnp.float32,
        )
    keyval_grad = jnp.zeros((D, 2 * D), jnp.float32)
    keyval_grad = lax.dynamic_update_slice_in_dim(keyval_grad, key_grad, seq_rank * head_width, 1)
    keyval_grad = lax.dynamic_update_slice_in_dim(
        keyval_grad, value_grad, D + seq_rank * head_width, 1
    )
    enc_long = product_t(cross_parts[0][1], key_cols) + product_t(cross_parts[0][2], value_cols)
    enc_short = product_t(cross_parts[1][1], key_cols) + product_t(cross_parts[1][2], value_cols)
    summed_long, summed_short = (
        lax.psum_scatter(
            enc_long.astype(jnp.bfloat16), "seq", scatter_dimension=1, tiled=True
        ).astype(jnp.float32),
        lax.psum_scatter(
            enc_short.astype(jnp.bfloat16), "seq", scatter_dimension=1, tiled=True
        ).astype(jnp.float32),
    )
    enc_grads = (summed_long.astype(jnp.bfloat16), summed_short.astype(jnp.bfloat16))
    text_rows = TEXT // seq_count
    own_text = tuple(
        (lax.dynamic_slice_in_dim(words, seq_rank * text_rows, text_rows, 1) for words in texts)
    )
    text_grads = tuple((product_t(enc_grad, w_text) for enc_grad in enc_grads))
    text_proj_grad = jnp.zeros((ENC, D), jnp.float32)
    text_bias_grad = jnp.zeros((D,), jnp.float32)
    for bucket in range(2):
        text_proj_grad = text_proj_grad + jnp.einsum(
            "ite,itd->ed", own_text[bucket], enc_grads[bucket], preferred_element_type=jnp.float32
        )
        text_bias_grad = text_bias_grad + jnp.sum(enc_grads[bucket].astype(jnp.float32), (0, 1))
    self_branch = grad_after_self.astype(jnp.bfloat16)
    self_out_grad = weight_grad(self_rows, self_branch)
    long_do, short_do = to_items(product_t(self_branch, w_self).astype(jnp.bfloat16))
    out_heads = (
        lax.all_to_all(long_do, "seq", split_axis=2, concat_axis=1, tiled=True),
        lax.all_to_all(short_do, "seq", split_axis=2, concat_axis=1, tiled=True),
    )
    kept_heads = self_heads()
    self_parts = tuple(
        (
            attend_backward(
                *split_three(kept_heads[bucket]),
                masks_self[bucket],
                score_scale,
                head_view(out_heads[bucket], head_dim)
            )
            for bucket in range(2)
        )
    )
    stacked_long = jnp.stack(self_parts[0], 2)
    stacked_short = jnp.stack(self_parts[1], 2)
    long_qkv, short_qkv = (
        lax.all_to_all(stacked_long, "seq", split_axis=1, concat_axis=3, tiled=True),
        lax.all_to_all(stacked_short, "seq", split_axis=1, concat_axis=3, tiled=True),
    )
    qkv_rows = to_rows(long_qkv, short_qkv)
    qkv_grad = weight_grad(normed_self, qkv_rows)
    grad_first, gain_zero, shift_zero = norm_back(
        inputs, gains[0], shifts[0], product_t(qkv_rows, w_qkv)
    )
    input_grad = grad_after_self + grad_first
    grads = (
        qkv_grad,
        self_out_grad,
        cross_query_grad,
        keyval_grad,
        cross_out_grad,
        text_proj_grad,
        text_bias_grad,
        feed_in_grad,
        feed_out_grad,
        jnp.stack([gain_zero, gain_one, gain_two]),
        jnp.stack([shift_zero, shift_one, shift_two]),
    )
    shares = (
        lax.psum_scatter(
            grads[0].astype(jnp.bfloat16), "seq", scatter_dimension=0, tiled=True
        ).astype(jnp.float32),
        lax.psum_scatter(
            grads[1].astype(jnp.bfloat16), "seq", scatter_dimension=0, tiled=True
        ).astype(jnp.float32),
        lax.psum_scatter(
            grads[2].astype(jnp.bfloat16), "seq", scatter_dimension=0, tiled=True
        ).astype(jnp.float32),
        lax.psum_scatter(
            grads[3].astype(jnp.bfloat16), "seq", scatter_dimension=0, tiled=True
        ).astype(jnp.float32),
        lax.psum_scatter(
            grads[4].astype(jnp.bfloat16), "seq", scatter_dimension=0, tiled=True
        ).astype(jnp.float32),
        lax.psum_scatter(
            grads[5].astype(jnp.bfloat16), "seq", scatter_dimension=0, tiled=True
        ).astype(jnp.float32),
        lax.psum_scatter(
            grads[6].astype(jnp.bfloat16), "seq", scatter_dimension=0, tiled=True
        ).astype(jnp.float32),
        lax.psum_scatter(
            grads[7].astype(jnp.bfloat16), "seq", scatter_dimension=0, tiled=True
        ).astype(jnp.float32),
        lax.psum_scatter(
            grads[8].astype(jnp.bfloat16), "seq", scatter_dimension=0, tiled=True
        ).astype(jnp.float32),
        lax.psum_scatter(grads[9], "seq", scatter_dimension=1, tiled=True).astype(jnp.float32),
        lax.psum_scatter(grads[10], "seq", scatter_dimension=1, tiled=True).astype(jnp.float32),
    )
    totals = (
        lax.psum(shares[0].astype(jnp.bfloat16), "dp").astype(jnp.float32),
        lax.psum(shares[1].astype(jnp.bfloat16), "dp").astype(jnp.float32),
        lax.psum(shares[2].astype(jnp.bfloat16), "dp").astype(jnp.float32),
        lax.psum(shares[3].astype(jnp.bfloat16), "dp").astype(jnp.float32),
        lax.psum(shares[4].astype(jnp.bfloat16), "dp").astype(jnp.float32),
        lax.psum(shares[5].astype(jnp.bfloat16), "dp").astype(jnp.float32),
        lax.psum(shares[6].astype(jnp.bfloat16), "dp").astype(jnp.float32),
        lax.psum(shares[7].astype(jnp.bfloat16), "dp").astype(jnp.float32),
        lax.psum(shares[8].astype(jnp.bfloat16), "dp").astype(jnp.float32),
        lax.psum(shares[9].astype(jnp.bfloat16), "dp").astype(jnp.float32),
        lax.psum(shares[10].astype(jnp.bfloat16), "dp").astype(jnp.float32),
    )
    long_output, short_output = to_items(result.astype(jnp.bfloat16))
    long_input_grad, short_input_grad = to_items(input_grad)
    return (
        long_output,
        short_output,
        long_input_grad,
        short_input_grad,
        text_grads[0],
        text_grads[1],
        totals[0],
        totals[1],
        totals[2],
        totals[3],
        totals[4],
        totals[5],
        totals[6],
        totals[7],
        totals[8],
        totals[9],
        totals[10],
    )


STAGES = 4
PARTS = 4
ALL_AXES = ("dp", "seq")


def fits_item_plan(mesh):
    return dict(mesh.shape) == {"dp": PARTS, "seq": 2 * STAGES}


def partner(values):
    return lax.ppermute(values, "seq", [(rank, rank ^ 1) for rank in range(2 * STAGES)])


def next_stage(values):
    count = 2 * STAGES
    return lax.ppermute(values, "seq", [(rank, (rank + 2) % count) for rank in range(count)])


def across(values, second):
    pairs = []
    for group in range(PARTS):
        for rank in range(2 * STAGES):
            flip = 1 + rank % 2 if not second else 2 - rank % 2
            pairs.append((group * 2 * STAGES + rank, (group ^ flip) * 2 * STAGES + rank))
    return lax.ppermute(values, ALL_AXES, pairs)


def stage_exchange(blocks):
    groups = [[2 * stage + core for stage in range(STAGES)] for core in range(2)]
    return lax.all_to_all(
        blocks, "seq", split_axis=0, concat_axis=0, axis_index_groups=groups, tiled=True
    )


def part_of(group, core, slot):
    flips = (0, 1 + core, 2 - core, 3)
    return lax.bitwise_xor(group, flips[slot])


def kernel_params(limit=40 << 20):
    return pltpu.CompilerParams(vmem_limit_bytes=limit)


VMEM_SPEC = pl.BlockSpec(memory_space=pltpu.VMEM)
SMEM_SPEC = pl.BlockSpec(memory_space=pltpu.SMEM)
ANY_SPEC = pl.BlockSpec(memory_space=pl.ANY)


LANES = 512


def after(values, *others):
    return lax.optimization_barrier((values, *others))[0]


def run_moves(moves, sems):
    started = []
    for number, (source, target) in enumerate(moves):
        move = pltpu.make_async_copy(source, target, sems.at[number])
        move.start()
        started.append(move)
    for move in started:
        move.wait()


def move_call(place, operands, out_shapes, plan):
    n, m = len(operands), len(out_shapes)

    class Blank:
        @property
        def at(self):
            return self

        def __getitem__(self, _):
            return self

    count = len(plan((0, 0, 0), [Blank()] * n, [Blank()] * m))

    def kernel(place_ref, *refs):
        spots = (place_ref[0], place_ref[1], place_ref[2])
        run_moves(plan(spots, refs[:n], refs[n : n + m]), refs[n + m])

    return pl.pallas_call(
        kernel,
        out_shape=[jax.ShapeDtypeStruct(shape, jnp.bfloat16) for shape in out_shapes],
        in_specs=[SMEM_SPEC] + [ANY_SPEC] * n,
        out_specs=[ANY_SPEC] * m,
        scratch_shapes=[pltpu.SemaphoreType.DMA((count,))],
        compiler_params=kernel_params(16 << 20),
    )(place, *operands)


def aligned(value, unit):
    return value if isinstance(value, int) else pl.multiple_of(value, unit)


class Split:
    def __init__(self, matrix, width, halves=False):
        self.matrix, self.width, self.halves = matrix, width, halves
        self.rows = matrix.shape[0]
        self.count = matrix.shape[1] // 2 // LANES
        self.part_rows = self.rows * 2 // PARTS
        self.shape = (self.rows * 2 * STAGES, matrix.shape[1] // 2)


class Whole:
    def __init__(self, matrix):
        self.matrix = matrix
        self.rows = matrix.shape[0]
        self.count = matrix.shape[1] // LANES
        self.part_rows = self.rows // PARTS
        self.shape = (self.rows * STAGES, matrix.shape[1])


def cut_columns(place, splits):
    total = 0
    for entry in splits:
        entry.start = total
        total += entry.rows * entry.count

    def plan(spots, refs, outs):
        moves = []
        for ref, entry in zip(refs, splits):
            width = entry.width
            for j in range(entry.count * LANES // width):
                target = (
                    pl.ds(entry.start + j * width // LANES * entry.rows, entry.rows),
                    pl.ds(j * width % LANES, width),
                )
                for side, out in enumerate(outs):
                    core = spots[2] if side == 0 else 1 - spots[2]
                    column = core * LANES if entry.halves else (2 * j + core) * width
                    moves.append((ref.at[:, pl.ds(aligned(column, 128), width)], out.at[target]))
        return moves

    mine, others = move_call(
        place, [entry.matrix for entry in splits], [(total, LANES)] * 2, plan
    )
    return mine, partner(others)


def pack_parts(place, entries, packed):
    wholes = [entry for entry in entries if isinstance(entry, Whole)]
    total = 0
    for entry in entries:
        entry.offset = total
        total += entry.part_rows * entry.count
    operands = list(packed or ()) + [entry.matrix for entry in wholes]
    first = len(operands) - len(wholes)

    def sources(spots, refs, flipped):
        moves = []
        for entry in entries:
            size = entry.part_rows
            for j in range(entry.count):
                if isinstance(entry, Whole):
                    ref = refs[first + wholes.index(entry)]
                    row = aligned(spots[1] * size, size)
                    source = ref.at[pl.ds(row, size), pl.ds(j * LANES, LANES)]
                else:
                    row = entry.start + j * entry.rows + (spots[1] & 1) * size
                    source = refs[1 if flipped else 0].at[pl.ds(aligned(row, 16), size)]
                moves.append((source, (pl.ds(entry.offset + j * size, size),)))
        return moves

    n = len(operands)
    count = sum(entry.count for entry in entries)

    def kernel(place_ref, *refs):
        spots = (place_ref[0], place_ref[1], place_ref[2])
        out, sems = refs[n], refs[n + 1]
        other = lax.bitwise_xor(lax.shift_right_logical(spots[1], 1), spots[2])
        for flipped in range(2):

            @pl.when(other == flipped)
            def _():
                moves = sources(spots, refs, flipped == 1)
                run_moves([(source, out.at[target]) for source, target in moves], sems)

    return pl.pallas_call(
        kernel,
        out_shape=jax.ShapeDtypeStruct((total, LANES), jnp.bfloat16),
        in_specs=[SMEM_SPEC] + [ANY_SPEC] * n,
        out_specs=ANY_SPEC,
        scratch_shapes=[pltpu.SemaphoreType.DMA((count,))],
        compiler_params=kernel_params(16 << 20),
    )(place, *operands)


def stage_hops(mine):
    hops = []
    for _ in range(STAGES - 1):
        mine = next_stage(mine)
        hops.append(mine)
    return hops


def share_hops(hops):
    stack = jnp.stack(hops)
    first = across(stack, False)
    second = across(stack, True)
    return stack, first, second, across(first, True)


def assemble(place, entries, packed, shared):
    wholes = [entry for entry in entries if isinstance(entry, Whole)]
    operands = list(shared) + list(packed or ()) + [entry.matrix for entry in wholes]
    first = len(operands) - len(wholes)

    def plan(spots, refs, outs):
        stage, group, core = spots
        moves = []
        for out, entry in zip(outs, entries):
            size = entry.part_rows
            rows = size * PARTS
            for j in range(entry.count):
                lanes = pl.ds(j * LANES, LANES)
                if isinstance(entry, Whole):
                    moves.append(
                        (
                            refs[first + wholes.index(entry)].at[:, lanes],
                            out.at[pl.ds(aligned(stage * rows, rows), rows), lanes],
                        )
                    )
                else:
                    for side in range(2):
                        row = stage * rows + (core if side == 0 else 1 - core) * entry.rows
                        moves.append(
                            (
                                refs[4 + side].at[
                                    pl.ds(entry.start + j * entry.rows, entry.rows)
                                ],
                                out.at[pl.ds(aligned(row, entry.rows), entry.rows), lanes],
                            )
                        )
                for hop in range(1, STAGES):
                    source_stage = (stage + STAGES - hop) & (STAGES - 1)
                    for slot in range(PARTS):
                        part = group ^ (0, 1 + core, 2 - core, 3)[slot]
                        row = aligned(source_stage * rows + part * size, size)
                        moves.append(
                            (
                                refs[slot].at[hop - 1, pl.ds(entry.offset + j * size, size)],
                                out.at[pl.ds(row, size), lanes],
                            )
                        )
        return moves

    return move_call(place, operands, [entry.shape for entry in entries], plan)


def group_blocks(place, pairs, shape, sums=None):
    n = len(pairs)

    def kernel(place_ref, *refs):
        stage, group, core = place_ref[0], place_ref[1], place_ref[2]
        far_ref, near_ref = refs[-2:]
        for to_stage in range(STAGES):
            hop = (stage + STAGES - to_stage) & (STAGES - 1)
            results = []
            for number, (left, right, _) in enumerate(pairs):
                rows = left.shape[1] // STAGES
                results.append(
                    lax.dot_general(
                        refs[2 * number][:, to_stage * rows : (to_stage + 1) * rows],
                        refs[2 * number + 1][...],
                        (((0,), (0,)), ((), ())),
                        preferred_element_type=jnp.float32,
                    ).astype(jnp.bfloat16)
                )
            for part in range(PARTS):
                apart = group ^ part
                slot = jnp.where((core == 1) & (apart != 0) & (apart != 3), 3 - apart, apart)
                slot = jnp.asarray(slot, jnp.int32)

                def put(out_ref, index):
                    for result, (left, right, moves) in zip(results, pairs):
                        columns = right.shape[1] // PARTS
                        for first, count, row, lane in moves:
                            out_ref[index, hop, row : row + count, lane : lane + columns] = result[
                                first : first + count, part * columns : (part + 1) * columns
                            ]
                    if sums is not None:
                        for side in range(2):
                            row = shape[0] // 2 * (side + 1) - 16
                            lane = 256 * to_stage + 128 * side
                            out_ref[index, hop, row : row + 16, 0:128] = refs[2 * n][
                                part, :, lane : lane + 128
                            ]
                            out_ref[index, hop, row : row + 16, 128:] = jnp.zeros(
                                (16, shape[1] - 128), jnp.bfloat16
                            )

                @pl.when(slot >= 2)
                def _():
                    put(far_ref, slot - 2)

                @pl.when(slot < 2)
                def _():
                    put(near_ref, slot)

    operands = [array for left, right, _ in pairs for array in (left, right)]
    if sums is not None:
        operands.append(sums)
    return pl.pallas_call(
        kernel,
        out_shape=[jax.ShapeDtypeStruct((2, STAGES, *shape), jnp.bfloat16)] * 2,
        in_specs=[SMEM_SPEC] + [VMEM_SPEC] * len(operands),
        out_specs=[VMEM_SPEC] * 2,
        compiler_params=kernel_params(48 << 20),
    )(place, *operands)


def wide(values):
    return values.astype(jnp.float32)


def narrow(values):
    return values.astype(jnp.bfloat16)


def reduce_group(far, near):
    got = across(far, True)
    send = narrow(wide(near[1]) + wide(got[1]))
    kept = wide(near[0]) + wide(got[0])
    other = across(send, False)
    total = kept + wide(other)
    moving = next_stage(narrow(total[1]))
    moving = next_stage(narrow(total[2] + wide(moving)))
    moving = next_stage(narrow(total[3] + wide(moving)))
    return narrow(total[0] + wide(moving))


def finish(place, block, outs, sums=False):
    first = across(block, False)
    second = across(block, True)
    third = across(first, True)

    def kernel(place_ref, *refs):
        for slot in range(PARTS):
            part = part_of(place_ref[1], place_ref[2], slot)
            held = refs[slot]
            for out_ref, (_, moves) in zip(refs[PARTS:], outs):
                for index, size, start in moves:
                    column = pl.multiple_of(start(part), 128)
                    out_ref[:, pl.ds(column, size)] = held[index].astype(jnp.float32)
            if sums:
                tail = held[:, block.shape[1] - 16 :, 0:128].astype(jnp.float32)
                refs[-1][part] = tail[0] + tail[1]

    shapes = [shape for shape, _ in outs] + ([(PARTS, 16, 128)] if sums else [])
    return pl.pallas_call(
        kernel,
        out_shape=[jax.ShapeDtypeStruct(shape, jnp.float32) for shape in shapes],
        in_specs=[SMEM_SPEC] + [VMEM_SPEC] * PARTS,
        out_specs=[VMEM_SPEC] * len(shapes),
        compiler_params=kernel_params(),
    )(place, block, first, second, third)


def kept_scores(query, keys, valid, first_row, causal):
    scores = (
        lax.dot_general(
            query, keys, (((1,), (1,)), ((), ())), preferred_element_type=jnp.float32
        )
        * 0.125
    )
    keep = valid > 0
    if causal:
        rows = first_row + lax.broadcasted_iota(jnp.int32, scores.shape, 0)
        keep = keep & (lax.broadcasted_iota(jnp.int32, scores.shape, 1) <= rows)
    return jnp.where(keep, scores, masked_value)


def probabilities(scores):
    raised = jnp.exp(scores - jnp.max(scores, -1, keepdims=True))
    return raised / jnp.sum(raised, -1, keepdims=True)


def chunks_of(length, causal):
    if not causal:
        return [(0, length, None)]
    return [(start, 128, start + 128) for start in range(0, length, 128)]


def attend_kernel(causal, valid_ref, q_ref, k_ref, v_ref, out_ref):
    keys_count = k_ref.shape[0]
    for head in range(2):
        lanes = slice(64 * head, 64 * head + 64)
        for start, size, limit in chunks_of(q_ref.shape[0], causal):
            limit = limit or keys_count
            scores = kept_scores(
                q_ref[start : start + size, lanes],
                k_ref[:limit, lanes],
                valid_ref[:, :limit],
                start,
                causal,
            )
            weights = narrow(probabilities(scores))
            out_ref[start : start + size, lanes] = narrow(product(weights, v_ref[:limit, lanes]))


def attend_pair(valid, query, keys, values, causal):
    length, count = query[0].shape[0], keys[0].shape[0]
    return pl.pallas_call(
        partial(attend_kernel, causal),
        out_shape=jax.ShapeDtypeStruct((length, 512), jnp.bfloat16),
        grid=(4,),
        in_specs=[pl.BlockSpec((1, count), lambda pair: (0, 0))]
        + [
            pl.BlockSpec((size, 128), lambda pair, first=first: (0, first + pair))
            for size, first in (
                (length, query[1]),
                (count, keys[1]),
                (count, values[1]),
            )
        ],
        out_specs=pl.BlockSpec((length, 128), lambda pair: (0, pair)),
        compiler_params=kernel_params(),
    )(valid, query[0], keys[0], values[0])


def attend_back_kernel(causal, valid_ref, q_ref, k_ref, v_ref, do_ref, dq_ref, dk_ref, dv_ref, key_sum, value_sum):
    keys_count = k_ref.shape[0]
    for head in range(2):
        lanes = slice(64 * head, 64 * head + 64)
        key_sum[...] = jnp.zeros_like(key_sum)
        value_sum[...] = jnp.zeros_like(value_sum)
        for start, size, limit in chunks_of(q_ref.shape[0], causal):
            limit = limit or keys_count
            query = q_ref[start : start + size, lanes]
            keys = k_ref[:limit, lanes]
            grad_out = do_ref[start : start + size, lanes]
            scores = kept_scores(query, keys, valid_ref[:, :limit], start, causal)
            probs = probabilities(scores)
            grad_probs = product_t(grad_out, v_ref[:limit, lanes])
            centre = jnp.sum(probs * grad_probs, -1, keepdims=True)
            grad_scores = narrow(probs * (grad_probs - centre))
            value_sum[:limit] += weight_grad(narrow(probs), grad_out)
            key_sum[:limit] += weight_grad(grad_scores, query)
            dq_ref[start : start + size, lanes] = narrow(product(grad_scores, keys) * 0.125)
        dk_ref[:, lanes] = narrow(key_sum[...] * 0.125)
        dv_ref[:, lanes] = narrow(value_sum[...])


def attend_back_pair(valid, query, keys, values, grad_out, causal):
    length, count = query[0].shape[0], keys[0].shape[0]
    return pl.pallas_call(
        partial(attend_back_kernel, causal),
        out_shape=[
            jax.ShapeDtypeStruct((size, 512), jnp.bfloat16) for size in (length, count, count)
        ],
        grid=(4,),
        in_specs=[pl.BlockSpec((1, count), lambda pair: (0, 0))]
        + [
            pl.BlockSpec((size, 128), lambda pair, first=first: (0, first + pair))
            for size, first in (
                (length, query[1]),
                (count, keys[1]),
                (count, values[1]),
                (length, 0),
            )
        ],
        out_specs=[
            pl.BlockSpec((size, 128), lambda pair: (0, pair)) for size in (length, count, count)
        ],
        scratch_shapes=[pltpu.VMEM((count, 64), jnp.float32)] * 2,
        compiler_params=kernel_params(),
    )(valid, query[0], keys[0], values[0], grad_out)


def normalise(values):
    centred = values - jnp.mean(values, -1, keepdims=True)
    scale = lax.rsqrt(jnp.mean(centred * centred, -1, keepdims=True) + norm_eps)
    return centred * scale, scale


def normal_back(unit, scale, gain_row, incoming):
    scaled = incoming * gain_row
    mean_one = jnp.mean(scaled, -1, keepdims=True)
    mean_two = jnp.mean(scaled * unit, -1, keepdims=True)
    return scale * (scaled - mean_one - unit * mean_two)


def on_item_device(
    long_frames,
    short_frames,
    long_text,
    short_text,
    long_lengths,
    short_lengths,
    text_lengths,
    qkv_weight,
    self_out,
    cross_query,
    cross_keyval,
    cross_out,
    text_proj,
    text_bias,
    feed_in,
    feed_out,
    norm_gains,
    norm_shifts,
    long_cot,
    short_cot,
):
    rank, group = lax.axis_index("seq"), lax.axis_index("dp")
    stage, core = rank // 2, rank % 2
    place = jnp.stack([stage, group, core]).astype(jnp.int32)
    is_first = core == 0
    rows, short_rows = long_frames.shape[1], short_frames.shape[1]
    length = rows * 2 * STAGES
    text_count = long_text.shape[1]

    def by_core(mine, other):
        return jnp.where(is_first, mine, other), jnp.where(is_first, other, mine)

    def blocks_of(long_part, short_part):
        padded = jnp.pad(short_part, ((0, 0), (0, rows - short_rows), (0, 0)))
        return jnp.concatenate([long_part, padded], 0)

    half = D // 2
    qkv_entry = [Split(qkv_weight, 128)]
    qkv_packed = cut_columns(place, qkv_entry)
    qkv_hops = stage_hops(pack_parts(place, qkv_entry, qkv_packed))

    params = jnp.concatenate([norm_gains, norm_shifts, text_bias[None]], 0)
    params = jnp.pad(params, ((0, 9), (0, D - params.shape[1])))
    frames = jnp.concatenate(
        [blocks_of(long_frames, short_frames), jnp.broadcast_to(params, (STAGES, 16, D))], 1
    )
    frames = stage_exchange(after(frames, qkv_packed[1]))
    frames = jnp.stack(by_core(frames, partner(frames)), 1)
    inputs = wide(frames[:, :, :rows].reshape(length, D))
    small = wide(frames[:, :, rows : rows + 7, : D // 8].transpose(2, 0, 1, 3).reshape(7, D))
    gains, shifts, bias = small[0:3], small[3:6], small[6]

    splits = [
        Split(after(cross_query, qkv_packed[1]), 128),
        Split(cross_keyval, 128),
        Split(text_proj, LANES, True),
        Split(feed_in, 512),
    ]
    packed = cut_columns(place, splits)
    (w_qkv,) = assemble(place, qkv_entry, qkv_packed, share_hops(qkv_hops))

    middle_entry = [Whole(self_out), *splits[:3], Whole(cross_out)]
    mine = pack_parts(place, middle_entry, packed)
    middle_hops = stage_hops(after(mine, qkv_hops[1]))
    w_self, w_query, w_keyval, w_text, w_cross = assemble(
        place, middle_entry, packed, share_hops(middle_hops)
    )
    in_entry = [splits[3]]
    in_hops = stage_hops(after(pack_parts(place, in_entry, packed), middle_hops[1]))
    (w_in,) = assemble(place, in_entry, packed, share_hops(in_hops))
    out_entry = [Whole(feed_out)]
    out_hops = stage_hops(after(pack_parts(place, out_entry, None), in_hops[1]))
    (w_out,) = assemble(place, out_entry, None, share_hops(out_hops))

    cots = stage_exchange(after(blocks_of(long_cot, short_cot), out_hops[0]))
    cots = jnp.stack(by_core(cots, partner(cots)), 1).reshape(length, D)

    spots = jnp.arange(length)
    real_rows = jnp.where(stage < STAGES // 2, rows, short_rows)
    frame_limit = lax.dynamic_index_in_dim(
        jnp.concatenate([long_lengths, short_lengths]), stage, keepdims=False
    )
    inside = spots % rows < real_rows
    valid = inside & ((spots // rows) * real_rows + spots % rows < frame_limit)
    valid = valid.astype(jnp.float32)[None]
    text_limit = lax.dynamic_index_in_dim(
        jnp.concatenate([text_lengths[0], text_lengths[1]]), stage, keepdims=False
    )
    text_valid = (jnp.arange(text_count) < text_limit).astype(jnp.float32)[None]
    words = lax.dynamic_index_in_dim(
        jnp.concatenate([long_text, short_text], 0), stage, keepdims=False
    )

    def pair_sum(part):
        return part + wide(partner(narrow(part)))

    unit0, scale0 = normalise(inputs)
    normed0 = narrow(unit0 * gains[0] + shifts[0])
    qkv = narrow(product(normed0, w_qkv))
    mixed = attend_pair(valid, (qkv, 0), (qkv, 4), (qkv, 8), True)
    after_self = inputs + pair_sum(product(mixed, w_self))
    unit1, scale1 = normalise(after_self)
    normed1 = narrow(unit1 * gains[1] + shifts[1])
    query = narrow(product(normed1, w_query))
    bias_mine = lax.dynamic_slice_in_dim(bias, core * half, half)
    encoded = narrow(product(words, w_text) + bias_mine)
    encoded = jnp.concatenate(by_core(encoded, partner(encoded)), 1)
    keyval = narrow(product(encoded, w_keyval))
    cross = attend_pair(text_valid, (query, 0), (keyval, 0), (keyval, 4), False)
    after_cross = after_self + pair_sum(product(cross, w_cross))
    unit2, scale2 = normalise(after_cross)
    normed2 = narrow(unit2 * gains[2] + shifts[2])
    pre_act = product(normed2, w_in)
    hidden = narrow(jax.nn.gelu(pre_act, approximate=False))

    def split_rows(values):
        parts = values.reshape(STAGES, 2, rows, D)
        mine = lax.dynamic_index_in_dim(parts, core, 1, keepdims=False)
        other = lax.dynamic_index_in_dim(parts, 1 - core, 1, keepdims=False)
        return mine, other

    def back_to_frames(values):
        moved = stage_exchange(narrow(values))
        return moved[: STAGES // 2], moved[STAGES // 2 :, :short_rows]

    out_mine, out_other = split_rows(product(hidden, w_out))
    base_mine, _ = split_rows(after_cross)
    long_output, short_output = back_to_frames(
        base_mine + out_mine + wide(partner(narrow(out_other)))
    )

    def own_rows(block):
        cut = block.reshape(2, block.shape[0] // 2, block.shape[1])
        mine = lax.dynamic_index_in_dim(cut, core, 0, keepdims=False)
        other = lax.dynamic_index_in_dim(cut, 1 - core, 0, keepdims=False)
        return jnp.stack(by_core(mine, partner(other)))

    hidden_rows = feed_out.shape[0]
    feed_out_block = reduce_group(
        *group_blocks(place, [(hidden, cots, [(0, hidden_rows, 0, 0)])], (hidden_rows, 256))
    )
    _, gelu_pull = jax.vjp(partial(jax.nn.gelu, approximate=False), pre_act)
    grad_pre = narrow(gelu_pull(product_t(cots, w_out))[0])
    feed_in_block = reduce_group(
        *group_blocks(place, [(normed2, grad_pre, [(0, 256, 0, 0)])], (256, 512))
    )
    part2 = product_t(grad_pre, w_in)
    grad_norm2 = pair_sum(part2)
    grad_after_cross = wide(cots) + normal_back(unit2, scale2, gains[2], grad_norm2)
    branch2 = narrow(grad_after_cross)
    grad_cross = narrow(product_t(branch2, w_cross))
    grad_query, grad_key, grad_value = attend_back_pair(
        text_valid, (query, 0), (keyval, 0), (keyval, 4), grad_cross, False
    )
    part1 = product_t(grad_query, w_query)
    grad_norm1 = pair_sum(part1)
    grad_after_self = grad_after_cross + normal_back(unit1, scale1, gains[1], grad_norm1)
    grad_keyval = jnp.concatenate([grad_key, grad_value], 1)
    grad_encoded = narrow(pair_sum(product_t(grad_keyval, w_keyval)))
    grad_encoded_mine = lax.dynamic_slice_in_dim(grad_encoded, core * half, half, 1)
    text_rows = ENC // (2 * STAGES)
    words_padded = jnp.pad(
        words.reshape(text_count, 2 * STAGES, text_rows), ((0, 0), (0, 0), (0, 128 - text_rows))
    ).reshape(text_count, D)
    grad_words = product_t(grad_encoded_mine, w_text).reshape(STAGES, 2, -1, ENC)
    words_mine = lax.dynamic_index_in_dim(grad_words, core, 1, keepdims=False)
    words_other = lax.dynamic_index_in_dim(grad_words, 1 - core, 1, keepdims=False)
    moved = wide(stage_exchange(narrow(words_mine + wide(partner(narrow(words_other))))))
    long_text_grad, short_text_grad = moved[: STAGES // 2], moved[STAGES // 2 :]

    branch1 = narrow(grad_after_self)
    middle_block = reduce_group(
        *group_blocks(
            place,
            [
                (cross, branch2, [(0, 128, 0, 0)]),
                (mixed, branch1, [(0, 128, 128, 0)]),
                (normed1, grad_query, [(0, 256, 256, 0)]),
                (words_padded, grad_encoded_mine, [(0, 256, 256, 128)]),
                (encoded, grad_keyval, [(0, 256, 512, 0)]),
            ],
            (768, 256),
        )
    )
    grad_mixed = narrow(product_t(branch1, w_self))
    grad_qkv = jnp.concatenate(
        attend_back_pair(valid, (qkv, 0), (qkv, 4), (qkv, 8), grad_mixed, True), 1
    )
    part0 = product_t(grad_qkv, w_qkv)
    sums = jnp.stack(
        [
            jnp.sum(part0 * unit0, 0),
            jnp.sum(part1 * unit1, 0),
            jnp.sum(part2 * unit2, 0),
            jnp.sum(part0, 0),
            jnp.sum(part1, 0),
            jnp.sum(part2, 0),
            0.5 * jnp.sum(wide(grad_encoded), 0),
            jnp.zeros((D,), jnp.float32),
        ]
    )
    sums = jnp.pad(narrow(sums).reshape(PARTS, 2, D), ((0, 0), (0, 14), (0, 0)))
    qkv_block = reduce_group(
        *group_blocks(
            place,
            [(normed0, grad_qkv, [(0, 128, 0, 0), (128, 128, 144, 0)])],
            (288, 384),
            sums,
        )
    )
    norm0_mine, norm0_other = split_rows(part0)
    grad_norm0 = norm0_mine + wide(partner(narrow(norm0_other)))
    unit0_mine, _ = split_rows(unit0)
    after_self_mine, _ = split_rows(grad_after_self)
    scale0_mine = lax.dynamic_index_in_dim(
        scale0.reshape(STAGES, 2, rows, 1), core, 1, keepdims=False
    )
    grad_inputs = after_self_mine + normal_back(unit0_mine, scale0_mine, gains[0], grad_norm0)
    long_input_grad, short_input_grad = back_to_frames(grad_inputs)

    shard = D // 8
    (feed_out_grad,) = finish(
        place, feed_out_block, [(feed_out.shape, [(..., 256, lambda part: part * 256)])]
    )

    def interleaved(width):
        return [
            ((side,), width, lambda part, side=side: (2 * part + side) * width) for side in range(2)
        ]

    (feed_in_grad,) = finish(place, own_rows(feed_in_block), [(feed_in.shape, interleaved(512))])
    sides = own_rows(
        middle_block[2 * shard :].reshape(2, 2, shard, 256).transpose(1, 0, 2, 3).reshape(4 * shard, 256)
    )
    sides = sides.reshape(4 * shard, 256)
    middle_block = jnp.concatenate([middle_block[: 2 * shard], sides], 0)

    def rows_at(first, count=shard, lanes=slice(None)):
        return (slice(first, first + count), lanes)

    cross_out_grad, self_out_grad, cross_query_grad, text_proj_grad, cross_keyval_grad = finish(
        place,
        middle_block,
        [
            (cross_out.shape, [(rows_at(0), 256, lambda part: part * 256)]),
            (self_out.shape, [(rows_at(shard), 256, lambda part: part * 256)]),
            (
                cross_query.shape,
                [
                    (
                        rows_at((2 + 2 * side) * shard, shard, slice(0, 128)),
                        128,
                        lambda part, side=side: (2 * part + side) * 128,
                    )
                    for side in range(2)
                ],
            ),
            (
                text_proj.shape,
                [
                    (
                        rows_at((2 + 2 * side) * shard, text_rows, slice(128, 256)),
                        128,
                        lambda part, side=side: side * half + part * 128,
                    )
                    for side in range(2)
                ],
            ),
            (
                cross_keyval.shape,
                [
                    (
                        rows_at((3 + 2 * side) * shard, shard, slice(128 * j, 128 * j + 128)),
                        128,
                        lambda part, side=side, j=j: (2 * (2 * part + j) + side) * 128,
                    )
                    for side in range(2)
                    for j in range(2)
                ],
            ),
        ],
    )
    qkv_grad, sums = finish(
        place,
        own_rows(qkv_block),
        [
            (
                qkv_weight.shape,
                [
                    (
                        (side, slice(0, shard), slice(128 * j, 128 * j + 128)),
                        128,
                        lambda part, side=side, j=j: (2 * (3 * part + j) + side) * 128,
                    )
                    for side in range(2)
                    for j in range(3)
                ],
            )
        ],
        True,
    )
    sums = sums[:, :2].reshape(8, shard)
    return (
        long_output,
        short_output,
        wide(long_input_grad),
        wide(short_input_grad),
        long_text_grad,
        short_text_grad,
        qkv_grad,
        self_out_grad,
        cross_query_grad,
        cross_keyval_grad,
        cross_out_grad,
        text_proj_grad,
        sums[6],
        feed_in_grad,
        feed_out_grad,
        sums[0:3],
        sums[3:6],
    )


def solution(mesh):
    return jax.shard_map(
        on_item_device if fits_item_plan(mesh) else on_device,
        mesh=mesh,
        in_specs=(
            P("dp", "seq", None),
            P("dp", "seq", None),
            P("dp", None, None),
            P("dp", None, None),
            P("dp"),
            P("dp"),
            P(None, "dp"),
            P("seq", None),
            P("seq", None),
            P("seq", None),
            P("seq", None),
            P("seq", None),
            P("seq", None),
            P("seq"),
            P("seq", None),
            P("seq", None),
            P(None, "seq"),
            P(None, "seq"),
            P("dp", "seq", None),
            P("dp", "seq", None),
        ),
        out_specs=(
            P("dp", "seq", None),
            P("dp", "seq", None),
            P("dp", "seq", None),
            P("dp", "seq", None),
            P("dp", "seq", None),
            P("dp", "seq", None),
            P("seq", None),
            P("seq", None),
            P("seq", None),
            P("seq", None),
            P("seq", None),
            P("seq", None),
            P("seq"),
            P("seq", None),
            P("seq", None),
            P(None, "seq"),
            P(None, "seq"),
        ),
        check_vma=False,
    )
```

```python
from functools import partial

import jax
import jax.numpy as jnp
from jax import lax
from jax.experimental import pallas as pl
from jax.experimental.pallas import tpu as pltpu
from jax.sharding import PartitionSpec as P

D = 1024
HEADS = 16
ENC = 768
TEXT = 64


masked_value = -1e30
norm_eps = 1e-05


def layer_norm(values, gain_row, bias_row):
    average = jnp.mean(values, -1, keepdims=True)
    centred = values - average
    spread = jnp.mean(centred * centred, -1, keepdims=True)
    return centred * lax.rsqrt(spread + norm_eps) * gain_row + bias_row


def norm_back(values, gain_row, bias_row, incoming):
    _, pullback = jax.vjp(layer_norm, values, gain_row, bias_row)
    return pullback(incoming)


def product(left, right):
    return jnp.dot(left, right, preferred_element_type=jnp.float32)


def product_t(left, right):
    return lax.dot_general(
        left, right, (((left.ndim - 1,), (1,)), ((), ())), preferred_element_type=jnp.float32
    )


def weight_grad(left, right):
    return lax.dot_general(
        left, right, (((0,), (0,)), ((), ())), preferred_element_type=jnp.float32
    )


def head_view(packed, head_dim):
    return packed.reshape(packed.shape[0], packed.shape[1], -1, head_dim)


def flatten_heads(tensor):
    return tensor.reshape(tensor.shape[0], tensor.shape[1], -1).astype(jnp.bfloat16)


def softmax_weights(query, keys, mask, score_scale):
    scores = (
        jnp.einsum("iqhd,ikhd->ihqk", query, keys, preferred_element_type=jnp.float32) * score_scale
    )
    scores = jnp.where(mask, scores, masked_value)
    row_max = jnp.max(scores, -1, keepdims=True)
    raised = jnp.exp(scores - row_max)
    return raised / jnp.sum(raised, -1, keepdims=True)


def attend_forward(query, keys, values, mask, score_scale):
    weights = softmax_weights(query, keys, mask, score_scale).astype(jnp.bfloat16)
    mixed = jnp.einsum("ihqk,ikhd->iqhd", weights, values, preferred_element_type=jnp.float32)
    return flatten_heads(mixed)


def attend_backward(query, keys, values, mask, score_scale, grad_out):
    probs = softmax_weights(query, keys, mask, score_scale)
    grad_values = jnp.einsum(
        "ihqk,iqhd->ikhd", probs.astype(jnp.bfloat16), grad_out, preferred_element_type=jnp.float32
    )
    grad_probs = jnp.einsum("iqhd,ikhd->ihqk", grad_out, values, preferred_element_type=jnp.float32)
    centre = jnp.sum(probs * grad_probs, -1, keepdims=True)
    grad_scores = (probs * (grad_probs - centre)).astype(jnp.bfloat16)
    grad_query = (
        jnp.einsum("ihqk,ikhd->iqhd", grad_scores, keys, preferred_element_type=jnp.float32)
        * score_scale
    )
    grad_keys = (
        jnp.einsum("ihqk,iqhd->ikhd", grad_scores, query, preferred_element_type=jnp.float32)
        * score_scale
    )
    return (flatten_heads(grad_query), flatten_heads(grad_keys), flatten_heads(grad_values))


def on_device(
    long_frames,
    short_frames,
    long_text,
    short_text,
    long_lengths,
    short_lengths,
    text_lengths,
    qkv_weight,
    self_out,
    cross_query,
    cross_keyval,
    cross_out,
    text_proj,
    text_bias,
    feed_in,
    feed_out,
    norm_gains,
    norm_shifts,
    long_cot,
    short_cot,
):
    w_qkv, w_self, w_query, w_keyval, w_cross, w_text, b_text, w_in, w_out, gains, shifts = (
        lax.all_gather(qkv_weight, "seq", axis=0, tiled=True),
        lax.all_gather(self_out, "seq", axis=0, tiled=True),
        lax.all_gather(cross_query, "seq", axis=0, tiled=True),
        lax.all_gather(cross_keyval, "seq", axis=0, tiled=True),
        lax.all_gather(cross_out, "seq", axis=0, tiled=True),
        lax.all_gather(text_proj, "seq", axis=0, tiled=True),
        lax.all_gather(text_bias, "seq", axis=0, tiled=True),
        lax.all_gather(feed_in, "seq", axis=0, tiled=True),
        lax.all_gather(feed_out, "seq", axis=0, tiled=True),
        lax.all_gather(norm_gains, "seq", axis=1, tiled=True),
        lax.all_gather(norm_shifts, "seq", axis=1, tiled=True),
    )
    seq_count = lax.axis_size("seq")
    seq_rank = lax.axis_index("seq")
    head_dim = D // HEADS
    head_width = D // seq_count
    score_scale = head_dim ** (-0.5)
    item_count, long_rows, _ = long_frames.shape
    short_rows = short_frames.shape[1]
    long_total = item_count * long_rows
    long_len = long_rows * seq_count
    short_len = short_rows * seq_count

    def to_items(joined):
        last_dim = joined.shape[-1]
        return (
            joined[:long_total].reshape(item_count, long_rows, last_dim),
            joined[long_total:].reshape(item_count, short_rows, last_dim),
        )

    def to_rows(long_part, short_part):
        return jnp.concatenate(
            [
                long_part.reshape(long_part.shape[0] * long_part.shape[1], -1),
                short_part.reshape(short_part.shape[0] * short_part.shape[1], -1),
            ],
            0,
        )

    def self_mask(lengths, full):
        places = jnp.arange(full)
        causal = places[:, None] >= places[None, :]
        return causal[None, None] & (places[None, None, None, :] < lengths[:, None, None, None])

    def text_mask(lengths):
        places = jnp.arange(TEXT)
        return (places[None, :] < lengths[:, None])[:, None, None, :]

    def split_three(packed):
        return (
            head_view(packed[:, :, 0], head_dim),
            head_view(packed[:, :, 1], head_dim),
            head_view(packed[:, :, 2], head_dim),
        )

    masks_self = (self_mask(long_lengths, long_len), self_mask(short_lengths, short_len))
    masks_text = (text_mask(text_lengths[0]), text_mask(text_lengths[1]))
    inputs = to_rows(long_frames, short_frames).astype(jnp.float32)
    normed_self = layer_norm(inputs, gains[0], shifts[0]).astype(jnp.bfloat16)

    def self_heads():
        packed = product(normed_self, w_qkv).astype(jnp.bfloat16)
        long_part, short_part = to_items(packed)
        long_part = long_part.reshape(item_count, long_rows, 3, D)
        short_part = short_part.reshape(item_count, short_rows, 3, D)
        return (
            lax.all_to_all(long_part, "seq", split_axis=3, concat_axis=1, tiled=True),
            lax.all_to_all(short_part, "seq", split_axis=3, concat_axis=1, tiled=True),
        )

    heads_pair = self_heads()
    long_mixed = attend_forward(*split_three(heads_pair[0]), masks_self[0], score_scale)
    short_mixed = attend_forward(*split_three(heads_pair[1]), masks_self[1], score_scale)
    long_back, short_back = (
        lax.all_to_all(long_mixed, "seq", split_axis=1, concat_axis=2, tiled=True),
        lax.all_to_all(short_mixed, "seq", split_axis=1, concat_axis=2, tiled=True),
    )
    self_rows = to_rows(long_back, short_back)
    after_self = inputs + product(self_rows, w_self)
    normed_cross = layer_norm(after_self, gains[1], shifts[1]).astype(jnp.bfloat16)
    long_query, short_query = to_items(product(normed_cross, w_query).astype(jnp.bfloat16))
    query_heads = (
        lax.all_to_all(long_query, "seq", split_axis=2, concat_axis=1, tiled=True),
        lax.all_to_all(short_query, "seq", split_axis=2, concat_axis=1, tiled=True),
    )
    key_cols = lax.dynamic_slice_in_dim(w_keyval, seq_rank * head_width, head_width, 1)
    value_cols = lax.dynamic_slice_in_dim(w_keyval, D + seq_rank * head_width, head_width, 1)
    texts = (long_text, short_text)
    encoded = tuple(((product(words, w_text) + b_text).astype(jnp.bfloat16) for words in texts))
    text_keys = tuple((product(enc_rows, key_cols).astype(jnp.bfloat16) for enc_rows in encoded))
    text_values = tuple(
        (product(enc_rows, value_cols).astype(jnp.bfloat16) for enc_rows in encoded)
    )
    cross_long = attend_forward(
        head_view(query_heads[0], head_dim),
        head_view(text_keys[0], head_dim),
        head_view(text_values[0], head_dim),
        masks_text[0],
        score_scale,
    )
    cross_short = attend_forward(
        head_view(query_heads[1], head_dim),
        head_view(text_keys[1], head_dim),
        head_view(text_values[1], head_dim),
        masks_text[1],
        score_scale,
    )
    cross_back_long, cross_back_short = (
        lax.all_to_all(cross_long, "seq", split_axis=1, concat_axis=2, tiled=True),
        lax.all_to_all(cross_short, "seq", split_axis=1, concat_axis=2, tiled=True),
    )
    cross_rows = to_rows(cross_back_long, cross_back_short)
    after_cross = after_self + product(cross_rows, w_cross)
    normed_feed = layer_norm(after_cross, gains[2], shifts[2]).astype(jnp.bfloat16)
    pre_act = product(normed_feed, w_in)
    hidden = jax.nn.gelu(pre_act, approximate=False).astype(jnp.bfloat16)
    result = after_cross + product(hidden, w_out)
    grad_rows = to_rows(long_cot, short_cot)
    feed_out_grad = weight_grad(hidden, grad_rows)
    _, gelu_pull = jax.vjp(partial(jax.nn.gelu, approximate=False), pre_act)
    grad_pre = gelu_pull(product_t(grad_rows, w_out))[0].astype(jnp.bfloat16)
    feed_in_grad = weight_grad(normed_feed, grad_pre)
    grad_cross_in, gain_two, shift_two = norm_back(
        after_cross, gains[2], shifts[2], product_t(grad_pre, w_in)
    )
    grad_after_cross = grad_rows.astype(jnp.float32) + grad_cross_in
    cross_branch = grad_after_cross.astype(jnp.bfloat16)
    cross_out_grad = weight_grad(cross_rows, cross_branch)
    long_dco, short_dco = to_items(product_t(cross_branch, w_cross).astype(jnp.bfloat16))
    grad_heads = (
        lax.all_to_all(long_dco, "seq", split_axis=2, concat_axis=1, tiled=True),
        lax.all_to_all(short_dco, "seq", split_axis=2, concat_axis=1, tiled=True),
    )
    cross_parts = tuple(
        (
            attend_backward(
                head_view(query_heads[bucket], head_dim),
                head_view(text_keys[bucket], head_dim),
                head_view(text_values[bucket], head_dim),
                masks_text[bucket],
                score_scale,
                head_view(grad_heads[bucket], head_dim),
            )
            for bucket in range(2)
        )
    )
    long_dq, short_dq = (
        lax.all_to_all(cross_parts[0][0], "seq", split_axis=1, concat_axis=2, tiled=True),
        lax.all_to_all(cross_parts[1][0], "seq", split_axis=1, concat_axis=2, tiled=True),
    )
    query_rows = to_rows(long_dq, short_dq)
    cross_query_grad = weight_grad(normed_cross, query_rows)
    grad_self_in, gain_one, shift_one = norm_back(
        after_self, gains[1], shifts[1], product_t(query_rows, w_query)
    )
    grad_after_self = grad_after_cross + grad_self_in
    key_grad = jnp.zeros((D, head_width), jnp.float32)
    value_grad = jnp.zeros((D, head_width), jnp.float32)
    for bucket in range(2):
        key_grad = key_grad + jnp.einsum(
            "itd,itw->dw",
            encoded[bucket],
            cross_parts[bucket][1],
            preferred_element_type=jnp.float32,
        )
        value_grad = value_grad + jnp.einsum(
            "itd,itw->dw",
            encoded[bucket],
            cross_parts[bucket][2],
            preferred_element_type=jnp.float32,
        )
    keyval_grad = jnp.zeros((D, 2 * D), jnp.float32)
    keyval_grad = lax.dynamic_update_slice_in_dim(keyval_grad, key_grad, seq_rank * head_width, 1)
    keyval_grad = lax.dynamic_update_slice_in_dim(
        keyval_grad, value_grad, D + seq_rank * head_width, 1
    )
    enc_long = product_t(cross_parts[0][1], key_cols) + product_t(cross_parts[0][2], value_cols)
    enc_short = product_t(cross_parts[1][1], key_cols) + product_t(cross_parts[1][2], value_cols)
    summed_long, summed_short = (
        lax.psum_scatter(
            enc_long.astype(jnp.bfloat16), "seq", scatter_dimension=1, tiled=True
        ).astype(jnp.float32),
        lax.psum_scatter(
            enc_short.astype(jnp.bfloat16), "seq", scatter_dimension=1, tiled=True
        ).astype(jnp.float32),
    )
    enc_grads = (summed_long.astype(jnp.bfloat16), summed_short.astype(jnp.bfloat16))
    text_rows = TEXT // seq_count
    own_text = tuple(
        (lax.dynamic_slice_in_dim(words, seq_rank * text_rows, text_rows, 1) for words in texts)
    )
    text_grads = tuple((product_t(enc_grad, w_text) for enc_grad in enc_grads))
    text_proj_grad = jnp.zeros((ENC, D), jnp.float32)
    text_bias_grad = jnp.zeros((D,), jnp.float32)
    for bucket in range(2):
        text_proj_grad = text_proj_grad + jnp.einsum(
            "ite,itd->ed", own_text[bucket], enc_grads[bucket], preferred_element_type=jnp.float32
        )
        text_bias_grad = text_bias_grad + jnp.sum(enc_grads[bucket].astype(jnp.float32), (0, 1))
    self_branch = grad_after_self.astype(jnp.bfloat16)
    self_out_grad = weight_grad(self_rows, self_branch)
    long_do, short_do = to_items(product_t(self_branch, w_self).astype(jnp.bfloat16))
    out_heads = (
        lax.all_to_all(long_do, "seq", split_axis=2, concat_axis=1, tiled=True),
        lax.all_to_all(short_do, "seq", split_axis=2, concat_axis=1, tiled=True),
    )
    kept_heads = self_heads()
    self_parts = tuple(
        (
            attend_backward(
                *split_three(kept_heads[bucket]),
                masks_self[bucket],
                score_scale,
                head_view(out_heads[bucket], head_dim)
            )
            for bucket in range(2)
        )
    )
    stacked_long = jnp.stack(self_parts[0], 2)
    stacked_short = jnp.stack(self_parts[1], 2)
    long_qkv, short_qkv = (
        lax.all_to_all(stacked_long, "seq", split_axis=1, concat_axis=3, tiled=True),
        lax.all_to_all(stacked_short, "seq", split_axis=1, concat_axis=3, tiled=True),
    )
    qkv_rows = to_rows(long_qkv, short_qkv)
    qkv_grad = weight_grad(normed_self, qkv_rows)
    grad_first, gain_zero, shift_zero = norm_back(
        inputs, gains[0], shifts[0], product_t(qkv_rows, w_qkv)
    )
    input_grad = grad_after_self + grad_first
    grads = (
        qkv_grad,
        self_out_grad,
        cross_query_grad,
        keyval_grad,
        cross_out_grad,
        text_proj_grad,
        text_bias_grad,
        feed_in_grad,
        feed_out_grad,
        jnp.stack([gain_zero, gain_one, gain_two]),
        jnp.stack([shift_zero, shift_one, shift_two]),
    )
    shares = (
        lax.psum_scatter(
            grads[0].astype(jnp.bfloat16), "seq", scatter_dimension=0, tiled=True
        ).astype(jnp.float32),
        lax.psum_scatter(
            grads[1].astype(jnp.bfloat16), "seq", scatter_dimension=0, tiled=True
        ).astype(jnp.float32),
        lax.psum_scatter(
            grads[2].astype(jnp.bfloat16), "seq", scatter_dimension=0, tiled=True
        ).astype(jnp.float32),
        lax.psum_scatter(
            grads[3].astype(jnp.bfloat16), "seq", scatter_dimension=0, tiled=True
        ).astype(jnp.float32),
        lax.psum_scatter(
            grads[4].astype(jnp.bfloat16), "seq", scatter_dimension=0, tiled=True
        ).astype(jnp.float32),
        lax.psum_scatter(
            grads[5].astype(jnp.bfloat16), "seq", scatter_dimension=0, tiled=True
        ).astype(jnp.float32),
        lax.psum_scatter(
            grads[6].astype(jnp.bfloat16), "seq", scatter_dimension=0, tiled=True
        ).astype(jnp.float32),
        lax.psum_scatter(
            grads[7].astype(jnp.bfloat16), "seq", scatter_dimension=0, tiled=True
        ).astype(jnp.float32),
        lax.psum_scatter(
            grads[8].astype(jnp.bfloat16), "seq", scatter_dimension=0, tiled=True
        ).astype(jnp.float32),
        lax.psum_scatter(grads[9], "seq", scatter_dimension=1, tiled=True).astype(jnp.float32),
        lax.psum_scatter(grads[10], "seq", scatter_dimension=1, tiled=True).astype(jnp.float32),
    )
    totals = (
        lax.psum(shares[0].astype(jnp.bfloat16), "dp").astype(jnp.float32),
        lax.psum(shares[1].astype(jnp.bfloat16), "dp").astype(jnp.float32),
        lax.psum(shares[2].astype(jnp.bfloat16), "dp").astype(jnp.float32),
        lax.psum(shares[3].astype(jnp.bfloat16), "dp").astype(jnp.float32),
        lax.psum(shares[4].astype(jnp.bfloat16), "dp").astype(jnp.float32),
        lax.psum(shares[5].astype(jnp.bfloat16), "dp").astype(jnp.float32),
        lax.psum(shares[6].astype(jnp.bfloat16), "dp").astype(jnp.float32),
        lax.psum(shares[7].astype(jnp.bfloat16), "dp").astype(jnp.float32),
        lax.psum(shares[8].astype(jnp.bfloat16), "dp").astype(jnp.float32),
        lax.psum(shares[9].astype(jnp.bfloat16), "dp").astype(jnp.float32),
        lax.psum(shares[10].astype(jnp.bfloat16), "dp").astype(jnp.float32),
    )
    long_output, short_output = to_items(result.astype(jnp.bfloat16))
    long_input_grad, short_input_grad = to_items(input_grad)
    return (
        long_output,
        short_output,
        long_input_grad,
        short_input_grad,
        text_grads[0],
        text_grads[1],
        totals[0],
        totals[1],
        totals[2],
        totals[3],
        totals[4],
        totals[5],
        totals[6],
        totals[7],
        totals[8],
        totals[9],
        totals[10],
    )


STAGES = 4
PARTS = 4
ALL_AXES = ("dp", "seq")


def fits_item_plan(mesh):
    return dict(mesh.shape) == {"dp": PARTS, "seq": 2 * STAGES}


def partner(values):
    return lax.ppermute(values, "seq", [(rank, rank ^ 1) for rank in range(2 * STAGES)])


def stage_shift(values, hop):
    count = 2 * STAGES
    pairs = [(rank, (rank + 2 * hop) % count) for rank in range(count)]
    return lax.ppermute(values, "seq", pairs)


def across(values, slot):
    pairs = []
    for group in range(PARTS):
        for rank in range(2 * STAGES):
            flip = (0, 1 + rank % 2, 2 - rank % 2, 3)[slot]
            pairs.append((group * 2 * STAGES + rank, (group ^ flip) * 2 * STAGES + rank))
    return lax.ppermute(values, ALL_AXES, pairs)


def stage_exchange(blocks):
    groups = [[2 * stage + core for stage in range(STAGES)] for core in range(2)]
    return lax.all_to_all(
        blocks, "seq", split_axis=0, concat_axis=0, axis_index_groups=groups, tiled=True
    )


def part_of(group, core, slot):
    flips = (0, 1 + core, 2 - core, 3)
    return lax.bitwise_xor(group, flips[slot])


def kernel_params(limit=40 << 20):
    return pltpu.CompilerParams(vmem_limit_bytes=limit)


RINGS = ('mid', 'qkv')
STAGE_FIRST = ('fo',)
ORDER = {'in<hops': ['frames'], 'out<hops': ['mid.third'], '<cots': ['out.hops'], '<frames': ['mid.hops', 'qkv.third'], 'mid<hops': ['qkv.hops'], 'in<cross': ['mid.third'], 'out<cross': ['in.third'], 'in.cross': 'query', 'cots': 'feed', 'in.third': 'cross', '<result': ['blocks'], 'fo.moving': 'late', 'fi.moving': 'late.got', 'cr.send': 'late.got', 'result': 'late.got', 'cr.moving': 'late.got', 'words': 'query'}
VMEM_SPEC = pl.BlockSpec(memory_space=pltpu.VMEM)
SMEM_SPEC = pl.BlockSpec(memory_space=pltpu.SMEM)
ANY_SPEC = pl.BlockSpec(memory_space=pl.ANY)
HBM_SPEC = pl.BlockSpec(memory_space=pltpu.HBM)


LANES = 512


def after(values, *others):
    return lax.optimization_barrier((values, *others))[0]


def run_moves(moves, sems):
    started = []
    for number, (source, target) in enumerate(moves):
        move = pltpu.make_async_copy(source, target, sems.at[number])
        move.start()
        started.append(move)
    for move in started:
        move.wait()


def move_call(place, operands, out_shapes, plan, raw=0):
    n, m = len(operands), len(out_shapes)

    class Blank:
        @property
        def at(self):
            return self

        def __getitem__(self, _):
            return self

    count = len(plan((0, 0, 0), [Blank()] * n, [Blank()] * m))

    def kernel(place_ref, *refs):
        spots = (place_ref[0], place_ref[1], place_ref[2])
        run_moves(plan(spots, refs[:n], refs[n : n + m]), refs[n + m])

    return pl.pallas_call(
        kernel,
        out_shape=[jax.ShapeDtypeStruct(shape, jnp.bfloat16) for shape in out_shapes],
        in_specs=[SMEM_SPEC] + [ANY_SPEC] * (n - raw) + [HBM_SPEC] * raw,
        out_specs=[ANY_SPEC] * m,
        scratch_shapes=[pltpu.SemaphoreType.DMA((count,))],
        compiler_params=kernel_params(16 << 20),
    )(place, *operands)


def aligned(value, unit):
    return value if isinstance(value, int) else pl.multiple_of(value, unit)


class Split:
    def __init__(self, matrix, width, halves=False):
        self.matrix, self.width, self.halves = matrix, width, halves
        self.rows = matrix.shape[0]
        self.count = matrix.shape[1] // 2 // LANES
        self.part_rows = self.rows * 2 // PARTS
        self.shape = (self.rows * 2 * STAGES, matrix.shape[1] // 2)


class Whole:
    def __init__(self, matrix):
        self.matrix = matrix
        self.rows = matrix.shape[0]
        self.count = matrix.shape[1] // LANES
        self.part_rows = self.rows // PARTS
        self.shape = (self.rows * STAGES, matrix.shape[1])


def cut_columns(place, splits):
    total = 0
    for entry in splits:
        entry.start = total
        total += entry.rows * entry.count

    def plan(spots, refs, outs):
        moves = []
        for ref, entry in zip(refs, splits):
            width = entry.width
            for j in range(entry.count * LANES // width):
                target = (
                    pl.ds(entry.start + j * width // LANES * entry.rows, entry.rows),
                    pl.ds(j * width % LANES, width),
                )
                for side, out in enumerate(outs):
                    core = spots[2] if side == 0 else 1 - spots[2]
                    column = core * LANES if entry.halves else (2 * j + core) * width
                    moves.append((ref.at[:, pl.ds(aligned(column, 128), width)], out.at[target]))
        return moves

    mine, others = move_call(
        place,
        [entry.matrix for entry in splits],
        [(total, LANES)] * 2,
        plan,
        len(splits),
    )
    return mine, partner(others)


def pack_parts(place, entries, packed):
    wholes = [entry for entry in entries if isinstance(entry, Whole)]
    total = 0
    for entry in entries:
        entry.offset = total
        total += entry.part_rows * entry.count
    operands = list(packed or ()) + [entry.matrix for entry in wholes]
    first = len(operands) - len(wholes)

    def sources(spots, refs, flipped):
        moves = []
        for entry in entries:
            size = entry.part_rows
            for j in range(entry.count):
                if isinstance(entry, Whole):
                    ref = refs[first + wholes.index(entry)]
                    row = aligned(spots[1] * size, size)
                    source = ref.at[pl.ds(row, size), pl.ds(j * LANES, LANES)]
                else:
                    row = entry.start + j * entry.rows + (spots[1] & 1) * size
                    source = refs[1 if flipped else 0].at[pl.ds(aligned(row, 16), size)]
                moves.append((source, (pl.ds(entry.offset + j * size, size),)))
        return moves

    n = len(operands)
    count = sum(entry.count for entry in entries)

    def kernel(place_ref, *refs):
        spots = (place_ref[0], place_ref[1], place_ref[2])
        out, sems = refs[n], refs[n + 1]
        other = lax.bitwise_xor(lax.shift_right_logical(spots[1], 1), spots[2])
        for flipped in range(2):

            @pl.when(other == flipped)
            def _():
                moves = sources(spots, refs, flipped == 1)
                run_moves([(source, out.at[target]) for source, target in moves], sems)

    return pl.pallas_call(
        kernel,
        out_shape=jax.ShapeDtypeStruct((total, LANES), jnp.bfloat16),
        in_specs=[SMEM_SPEC] + [ANY_SPEC] * first + [HBM_SPEC] * len(wholes),
        out_specs=ANY_SPEC,
        scratch_shapes=[pltpu.SemaphoreType.DMA((count,))],
        compiler_params=kernel_params(16 << 20),
    )(place, *operands)


def stage_hops(mine, ring):
    hops = []
    for hop in range(1, STAGES):
        hops.append(stage_shift(hops[-1] if ring and hops else mine, 1 if ring else hop))
    return hops


def assemble(place, entries, packed, shared):
    wholes = [entry for entry in entries if isinstance(entry, Whole)]
    operands = list(shared) + list(packed or ()) + [entry.matrix for entry in wholes]
    first = len(operands) - len(wholes)

    def plan(spots, refs, outs):
        stage, group, core = spots
        moves = []
        for out, entry in zip(outs, entries):
            size = entry.part_rows
            rows = size * PARTS
            for j in range(entry.count):
                lanes = pl.ds(j * LANES, LANES)
                if isinstance(entry, Whole):
                    moves.append(
                        (
                            refs[first + wholes.index(entry)].at[:, lanes],
                            out.at[pl.ds(aligned(stage * rows, rows), rows), lanes],
                        )
                    )
                else:
                    for side in range(2):
                        row = stage * rows + (core if side == 0 else 1 - core) * entry.rows
                        moves.append(
                            (
                                refs[4 + side].at[
                                    pl.ds(entry.start + j * entry.rows, entry.rows)
                                ],
                                out.at[pl.ds(aligned(row, entry.rows), entry.rows), lanes],
                            )
                        )
                for hop in range(1, STAGES):
                    source_stage = (stage + STAGES - hop) & (STAGES - 1)
                    for slot in range(PARTS):
                        part = group ^ (0, 1 + core, 2 - core, 3)[slot]
                        row = aligned(source_stage * rows + part * size, size)
                        moves.append(
                            (
                                refs[slot].at[hop - 1, pl.ds(entry.offset + j * size, size)],
                                out.at[pl.ds(row, size), lanes],
                            )
                        )
        return moves

    return move_call(place, operands, [entry.shape for entry in entries], plan, len(wholes))


def group_blocks(place, pairs, shape, sums=None, by_hop=False):
    n = len(pairs)
    out_shapes = [(PARTS, *shape)] * STAGES if by_hop else [(2, STAGES, *shape)] * 2
    outs = len(out_shapes)

    def kernel(place_ref, *refs):
        stage, group, core = place_ref[0], place_ref[1], place_ref[2]
        out_refs = refs[-outs:]
        for to_stage in range(STAGES):
            hop = (stage + STAGES - to_stage) & (STAGES - 1)
            results = []
            for number, (left, right, _) in enumerate(pairs):
                rows = left.shape[1] // STAGES
                results.append(
                    lax.dot_general(
                        refs[2 * number][:, to_stage * rows : (to_stage + 1) * rows],
                        refs[2 * number + 1][...],
                        (((0,), (0,)), ((), ())),
                        preferred_element_type=jnp.float32,
                    ).astype(jnp.bfloat16)
                )
            for part in range(PARTS):
                apart = group ^ part
                slot = jnp.where((core == 1) & (apart != 0) & (apart != 3), 3 - apart, apart)
                slot = jnp.asarray(slot, jnp.int32)

                def put(out_ref, *index):
                    for result, (left, right, moves) in zip(results, pairs):
                        columns = right.shape[1] // PARTS
                        for first, count, row, lane, *cut in moves:
                            start, size = cut or (0, columns)
                            spot = (slice(row, row + count), slice(lane, lane + size))
                            start += part * columns
                            out_ref[(*index, *spot)] = result[
                                first : first + count, start : start + size
                            ]
                    if sums is not None:
                        for side in range(2):
                            row = shape[0] - 16 - (1 - side) * 144
                            lane = 256 * to_stage + 128 * side
                            out_ref[(*index, slice(row, row + 16), slice(0, 128))] = refs[2 * n][
                                part, :, lane : lane + 128
                            ]
                            out_ref[(*index, slice(row, row + 16), slice(128, None))] = jnp.zeros(
                                (16, shape[1] - 128), jnp.bfloat16
                            )

                if by_hop:
                    for number in range(STAGES):

                        @pl.when(hop == number)
                        def _():
                            put(out_refs[number], slot)

                else:

                    @pl.when(slot >= 2)
                    def _():
                        put(out_refs[0], slot - 2, hop)

                    @pl.when(slot < 2)
                    def _():
                        put(out_refs[1], slot, hop)

    operands = [array for left, right, _ in pairs for array in (left, right)]
    if sums is not None:
        operands.append(sums)
    return pl.pallas_call(
        kernel,
        out_shape=[jax.ShapeDtypeStruct(one, jnp.bfloat16) for one in out_shapes],
        in_specs=[SMEM_SPEC] + [VMEM_SPEC] * len(operands),
        out_specs=[VMEM_SPEC] * outs,
        compiler_params=kernel_params(48 << 20),
    )(place, *operands)


def wide(values):
    return values.astype(jnp.float32)


def narrow(values):
    return values.astype(jnp.bfloat16)


class Order:
    def __init__(self):
        self.results = {}

    def note(self, name, *values):
        self.results[name] = values
        return values[0] if len(values) == 1 else values

    def step(self, name, value):
        waits = [
            value_of
            for key, values in self.results.items()
            if ORDER.get(key) == name
            for value_of in values
        ]
        return after(value, *waits) if waits else value

    def behind(self, name, value):
        waits = [
            one for key in ORDER.get(name, ()) if key in self.results for one in self.results[key]
        ]
        return after(value, *waits) if waits else value


class Reduction:
    def __init__(self, order, name, blocks):
        if name in STAGE_FIRST:
            self.stage_first(order, name, blocks)
            return
        far, near = blocks
        got = order.step(name + ".got", across(far, 2))
        self.send = order.note(name + ".send", narrow(wide(near[1]) + wide(got[1])))
        other = order.step(name + ".other", across(self.send, 1))
        total = [
            wide(near[0, hop]) + wide(got[0, hop]) + wide(other[hop]) for hop in range(STAGES)
        ]
        self.moving = order.note(
            name + ".moving", *[narrow(total[hop]) for hop in range(1, STAGES)]
        )
        moved = [stage_shift(self.moving[hop - 1], -hop) for hop in range(1, STAGES)]
        self.parts = [total[0], *moved]


    def stage_first(self, order, name, blocks):
        moving = stage_shift(blocks[1], 1)
        moving = stage_shift(narrow(wide(blocks[2]) + wide(moving)), 1)
        moving = stage_shift(narrow(wide(blocks[3]) + wide(moving)), 1)
        total = wide(blocks[0]) + wide(moving)
        far = order.note(name + ".moving", narrow(total[2:]))
        got = order.step(name + ".got", across(far, 2))
        self.send = order.note(name + ".send", narrow(total[1] + wide(got[1])))
        other = order.step(name + ".other", across(self.send, 1))
        self.parts = [total[0], got[0], other]

    def block(self):
        total, *rest = self.parts
        for part in rest:
            total = total + wide(part)
        return narrow(total)


def finish(place, block, outs, sums=()):
    first, second = across(block, 1), across(block, 2)
    third = across(first, 2)

    def kernel(place_ref, *refs):
        for slot in range(PARTS):
            part = part_of(place_ref[1], place_ref[2], slot)
            held = refs[slot]
            for out_ref, (_, moves) in zip(refs[PARTS:], outs):
                for index, size, start in moves:
                    column = pl.multiple_of(start(part), 128)
                    out_ref[:, pl.ds(column, size)] = held[index].astype(jnp.float32)
            if sums:
                first_sums, second_sums = (
                    held[row : row + 16, 0:128].astype(jnp.float32) for row in sums
                )
                refs[-1][part] = first_sums + second_sums

    shapes = [shape for shape, _ in outs] + ([(PARTS, 16, 128)] if sums else [])
    return pl.pallas_call(
        kernel,
        out_shape=[jax.ShapeDtypeStruct(shape, jnp.float32) for shape in shapes],
        in_specs=[SMEM_SPEC] + [VMEM_SPEC] * PARTS,
        out_specs=[VMEM_SPEC] * len(shapes),
        compiler_params=kernel_params(),
    )(place, block, first, second, third)


def lanes_of(values):
    return lax.broadcasted_iota(jnp.int32, values.shape, 1)


def of_head(values, head):
    return (lanes_of(values) >= 64) == (head == 1)


def with_terms(values, head, terms):
    out = jnp.where(of_head(values, head), values, 0.0)
    for number, term in enumerate(terms):
        out = jnp.where(lanes_of(values) == 64 * (1 - head) + number, term, out)
    return narrow(out)


def in_three(values):
    first = wide(narrow(values))
    second = wide(narrow(values - first))
    return first, second, wide(narrow(values - first - second))


def tiles_of(length, keys, size, causal):
    if not causal:
        return [(0, length, [(0, keys, False)])]
    tiles = []
    for start in range(0, length, size):
        count = min(size, length - start)
        runs = [(0, start, False)] if start else []
        tiles.append((start, count, runs + [(start, count, 2)]))
    return tiles


def causal_scores(scores, first_key, first_query, diagonal):
    if not diagonal:
        return scores
    key = first_key + lax.broadcasted_iota(jnp.int32, scores.shape, 0)
    query = first_query + lax.broadcasted_iota(jnp.int32, scores.shape, 1)
    return jnp.where(key <= query, scores, masked_value)


def attend_kernel(tiles, bias_ref, q_ref, k_ref, v_ref, out_ref, level_ref):
    query = wide(q_ref[...]) * 0.125
    keys, values = wide(k_ref[...]), wide(v_ref[...])
    bias = bias_ref[...]
    queries = [with_terms(query, head, [1.0]) for head in range(2)]
    keyed = [with_terms(keys, head, [bias]) for head in range(2)]
    turned = [
        jnp.transpose(narrow(jnp.where(of_head(values, head), values, 1.0))) for head in range(2)
    ]
    for start, size, runs in tiles:
        mixed, levels = [], []
        for head in range(2):
            scores = [
                causal_scores(
                    product_t(keyed[head][first : first + count], queries[head][start : start + size]),
                    first,
                    start,
                    diagonal,
                )
                for first, count, diagonal in runs
            ]
            top = jnp.max(scores[0], 0, keepdims=True)
            for more in scores[1:]:
                top = jnp.maximum(top, jnp.max(more, 0, keepdims=True))
            summed = None
            for part, (first, count, _) in zip(scores, runs):
                term = product(turned[head][:, first : first + count], narrow(jnp.exp(part - top)))
                summed = term if summed is None else summed + term
            weight = summed[64 * (1 - head) : 64 * (1 - head) + 1]
            mixed.append(summed[64 * head : 64 * head + 64] * (1.0 / weight))
            levels.append(jnp.broadcast_to(top + jnp.log(weight), (64, size)))
        out_ref[start : start + size, :] = narrow(jnp.transpose(jnp.concatenate(mixed, 0)))
        level_ref[start : start + size, :] = jnp.transpose(jnp.concatenate(levels[::-1], 0))


def pair_specs(bias, blocks):
    return [pl.BlockSpec(bias.shape, lambda pair: (0, 0))] + [
        pl.BlockSpec((size, 128), lambda pair, first=first: (0, first + pair))
        for size, first in blocks
    ]


def attend_pair(bias, query, keys, values, causal):
    length, count = query[0].shape[0], keys[0].shape[0]
    tiles = tiles_of(length, count, length, causal)
    return pl.pallas_call(
        partial(attend_kernel, tiles),
        out_shape=[
            jax.ShapeDtypeStruct((length, 512), jnp.bfloat16),
            jax.ShapeDtypeStruct((length, 512), jnp.float32),
        ],
        grid=(4,),
        in_specs=pair_specs(
            bias, [(length, query[1]), (count, keys[1]), (count, values[1])]
        ),
        out_specs=[pl.BlockSpec((length, 128), lambda pair: (0, pair))] * 2,
        compiler_params=kernel_params(),
    )(bias, query[0], keys[0], values[0])


def attend_back_kernel(
    tiles,
    bias_ref,
    q_ref,
    k_ref,
    v_ref,
    do_ref,
    out_ref,
    level_ref,
    dq_ref,
    dk_ref,
    dv_ref,
    key_sum,
    value_sum,
):
    query = wide(q_ref[...]) * 0.125
    keys, values, grad = wide(k_ref[...]), wide(v_ref[...]), wide(do_ref[...])
    bias = bias_ref[...]
    levels = in_three(-level_ref[...])
    centred = grad * wide(out_ref[...])
    plain_query, plain_grad = narrow(query), do_ref[...]
    turned = jnp.transpose(k_ref[...])
    last = tiles[-1][0]
    grads = []
    for head in range(2):
        centre = -jnp.sum(
            jnp.where(of_head(centred, head), centred, 0.0), -1, keepdims=True
        )
        centres = in_three(centre)
        queries = with_terms(query, head, [1.0, *levels])
        keyed = with_terms(keys, head, [bias, 1.0, 1.0, 1.0])
        outs = with_terms(grad, head, centres)
        valued = with_terms(values, head, [1.0, 1.0, 1.0])
        pieces = []
        for start, size, runs in reversed(tiles):
            rows = slice(start, start + size)
            summed = None
            for first, count, diagonal in runs:
                span = slice(first, first + count)
                probs = jnp.exp(
                    causal_scores(product_t(keyed[span], queries[rows]), first, start, diagonal)
                )
                grad_scores = narrow(probs * product_t(valued[span], outs[rows]))
                value_term = product(narrow(probs), plain_grad[rows])
                key_term = product(grad_scores, plain_query[rows])
                term = product(turned[:, span], grad_scores)
                summed = term if summed is None else summed + term
                if start == last:
                    value_sum[head, span] = value_term
                    key_sum[head, span] = key_term
                else:
                    value_sum[head, span] += value_term
                    key_sum[head, span] += key_term
            pieces.append(summed[64 * head : 64 * head + 64] * 0.125)
        grads.append(pieces)
    for (start, size, _), first, second in zip(reversed(tiles), *grads):
        dq_ref[start : start + size, :] = narrow(
            jnp.transpose(jnp.concatenate([first, second], 0))
        )
    of_second = of_head(keys, 1)
    dk_ref[...] = narrow(jnp.where(of_second, key_sum[1], key_sum[0]))
    dv_ref[...] = narrow(jnp.where(of_second, value_sum[1], value_sum[0]))


def attend_back_pair(bias, query, keys, values, grad_out, mixed, levels, causal):
    length, count = query[0].shape[0], keys[0].shape[0]
    tiles = tiles_of(length, count, 384, causal)
    return pl.pallas_call(
        partial(attend_back_kernel, tiles),
        out_shape=[
            jax.ShapeDtypeStruct((size, 512), jnp.bfloat16) for size in (length, count, count)
        ],
        grid=(4,),
        in_specs=pair_specs(
            bias,
            [(length, query[1]), (count, keys[1]), (count, values[1])] + [(length, 0)] * 3,
        ),
        out_specs=[
            pl.BlockSpec((size, 128), lambda pair: (0, pair)) for size in (length, count, count)
        ],
        scratch_shapes=[pltpu.VMEM((2, count, 128), jnp.float32)] * 2,
        compiler_params=kernel_params(),
    )(bias, query[0], keys[0], values[0], grad_out, mixed, levels)


def feed_kernel(rows_ref, weight_ref, hidden_ref, slope_ref):
    pre = product(rows_ref[...], weight_ref[...])
    below = 0.5 * (1.0 + lax.erf(pre * 0.7071067811865476))
    hidden_ref[...] = narrow(pre * below)
    slope_ref[...] = narrow(below + pre * jnp.exp(pre * pre * -0.5) * 0.3989422804014327)


def feed_forward(rows, weight):
    count, width = rows.shape[0], 512
    return pl.pallas_call(
        feed_kernel,
        out_shape=[jax.ShapeDtypeStruct((count, weight.shape[1]), jnp.bfloat16)] * 2,
        grid=(weight.shape[1] // width,),
        in_specs=[
            pl.BlockSpec((count, rows.shape[1]), lambda step: (0, 0)),
            pl.BlockSpec((weight.shape[0], width), lambda step: (0, step)),
        ],
        out_specs=[pl.BlockSpec((count, width), lambda step: (0, step))] * 2,
        compiler_params=kernel_params(),
    )(rows, weight)


def normalise(values):
    centred = values - jnp.mean(values, -1, keepdims=True)
    scale = lax.rsqrt(jnp.mean(centred * centred, -1, keepdims=True) + norm_eps)
    return centred * scale, scale


def normal_back(unit, scale, gain_row, incoming):
    scaled = incoming * gain_row
    mean_one = jnp.mean(scaled, -1, keepdims=True)
    mean_two = jnp.mean(scaled * unit, -1, keepdims=True)
    return scale * (scaled - mean_one - unit * mean_two)


def on_item_device(
    long_frames,
    short_frames,
    long_text,
    short_text,
    long_lengths,
    short_lengths,
    text_lengths,
    qkv_weight,
    self_out,
    cross_query,
    cross_keyval,
    cross_out,
    text_proj,
    text_bias,
    feed_in,
    feed_out,
    norm_gains,
    norm_shifts,
    long_cot,
    short_cot,
):
    rank, group = lax.axis_index("seq"), lax.axis_index("dp")
    stage, core = rank // 2, rank % 2
    place = jnp.stack([stage, group, core]).astype(jnp.int32)
    is_first = core == 0
    rows, short_rows = long_frames.shape[1], short_frames.shape[1]
    length = rows * 2 * STAGES
    text_count = long_text.shape[1]

    def by_core(mine, other):
        return jnp.where(is_first, mine, other), jnp.where(is_first, other, mine)

    def blocks_of(long_part, short_part):
        padded = jnp.pad(short_part, ((0, 0), (0, rows - short_rows), (0, 0)))
        return jnp.concatenate([long_part, padded], 0)

    half = D // 2
    order = Order()
    qkv_entry = [Split(qkv_weight, 128)]
    qkv_packed = cut_columns(place, qkv_entry)
    params = jnp.concatenate([norm_gains, norm_shifts, text_bias[None]], 0)
    params = jnp.pad(params, ((0, 9), (0, D - params.shape[1])))
    frames = jnp.concatenate(
        [blocks_of(long_frames, short_frames), jnp.broadcast_to(params, (STAGES, 16, D))], 1
    )

    def start_group(name, entries, packed):
        mine = order.behind(name + "<hops", pack_parts(place, entries, packed))
        return order.note(name + ".hops", *stage_hops(mine, name in RINGS))

    def cross_plane(name, hops):
        stack = order.behind(name + "<cross", jnp.stack(hops))
        first, second = order.note(name + ".cross", across(stack, 1), across(stack, 2))
        return stack, first, second

    def end_group(name, entries, packed, parts):
        stack, first, second = parts
        third = across(order.behind(name + "<third", after(first, second)), 2)
        order.note(name + ".third", third)
        return assemble(place, entries, packed, [stack, first, second, third])

    def move_frames():
        order.note("frames", stage_exchange(order.behind("<frames", frames)))

    def move_cots():
        order.note(
            "cots", stage_exchange(order.behind("<cots", blocks_of(long_cot, short_cot)))
        )

    qkv_hops = start_group("qkv", qkv_entry, qkv_packed)
    splits = [
        Split(after(cross_query, qkv_hops[0]), 128),
        Split(after(cross_keyval, qkv_hops[0]), 128),
        Split(after(text_proj, qkv_hops[0]), LANES, True),
        Split(after(feed_in, qkv_hops[0]), 512),
    ]
    packed = cut_columns(place, splits)
    middle_entry = [Whole(self_out), *splits[:3], Whole(cross_out)]
    qkv_parts = cross_plane("qkv", qkv_hops)
    middle_hops = start_group("mid", middle_entry, packed)
    (w_qkv,) = end_group("qkv", qkv_entry, qkv_packed, qkv_parts)
    move_frames()
    middle_parts = cross_plane("mid", middle_hops)
    in_group = ("in", [splits[3]], packed)
    out_group = ("out", [Whole(feed_out)], None)
    in_hops = start_group(*in_group)
    out_hops = start_group(*out_group)
    move_cots()

    (frames,) = order.results["frames"]
    frames_mine = frames[:, :rows]
    frames = jnp.stack(by_core(frames, partner(frames)), 1)
    inputs = wide(frames[:, :, :rows].reshape(length, D))
    small = wide(frames[:, :, rows : rows + 7, : D // 8].transpose(2, 0, 1, 3).reshape(7, D))
    gains, shifts, bias = small[0:3], small[3:6], small[6]

    spots = jnp.arange(length)
    real_rows = jnp.where(stage < STAGES // 2, rows, short_rows)
    frame_limit = lax.dynamic_index_in_dim(
        jnp.concatenate([long_lengths, short_lengths]), stage, keepdims=False
    )
    inside = spots % rows < real_rows
    valid = inside & ((spots // rows) * real_rows + spots % rows < frame_limit)
    key_bias = jnp.where(valid, 0.0, masked_value).astype(jnp.float32)[:, None]
    text_limit = lax.dynamic_index_in_dim(
        jnp.concatenate([text_lengths[0], text_lengths[1]]), stage, keepdims=False
    )
    text_bias_rows = jnp.where(jnp.arange(text_count) < text_limit, 0.0, masked_value)
    text_bias_rows = text_bias_rows.astype(jnp.float32)[:, None]
    words = lax.dynamic_index_in_dim(
        jnp.concatenate([long_text, short_text], 0), stage, keepdims=False
    )

    text_rows = ENC // (2 * STAGES)
    words_padded = jnp.pad(
        words.reshape(text_count, 2 * STAGES, text_rows), ((0, 0), (0, 0), (0, 128 - text_rows))
    ).reshape(text_count, D)
    order.note("words", words_padded)

    def pair_sum(part):
        return part + wide(partner(narrow(part)))

    unit0, scale0 = normalise(inputs)
    normed0 = narrow(unit0 * gains[0] + shifts[0])
    qkv = narrow(product(order.step("qkv", normed0), w_qkv))
    mixed, levels = attend_pair(
        key_bias, (order.step("attend", qkv), 0), (qkv, 4), (qkv, 8), True
    )
    order.note("mixed", mixed)
    w_self, w_query, w_keyval, w_text, w_cross = end_group(
        "mid", middle_entry, packed, middle_parts
    )
    in_parts = cross_plane("in", in_hops)
    after_self = inputs + order.step(
        "self.sum", pair_sum(product(order.step("self", mixed), w_self))
    )
    unit1, scale1 = normalise(after_self)
    normed1 = narrow(unit1 * gains[1] + shifts[1])
    query = narrow(product(order.step("query", normed1), w_query))
    bias_mine = lax.dynamic_slice_in_dim(bias, core * half, half)
    encoded = narrow(product(words, w_text) + bias_mine)
    encoded = jnp.concatenate(by_core(encoded, partner(encoded)), 1)
    keyval = narrow(product(encoded, w_keyval))
    cross, cross_levels = attend_pair(
        text_bias_rows, (query, 0), (keyval, 0), (keyval, 4), False
    )
    order.note("cross", cross)
    (w_in,) = end_group(*in_group, in_parts)
    out_parts = cross_plane("out", out_hops)
    after_cross = after_self + order.step(
        "cross.sum", pair_sum(product(order.step("cross", cross), w_cross))
    )
    unit2, scale2 = normalise(after_cross)
    normed2 = narrow(unit2 * gains[2] + shifts[2])
    hidden, slope = feed_forward(order.step("feed", normed2), w_in)
    order.note("hidden", hidden)
    (w_out,) = end_group(*out_group, out_parts)
    (cots,) = order.results["cots"]
    cots = jnp.stack(by_core(cots, partner(cots)), 1).reshape(length, D)

    def split_rows(values):
        parts = values.reshape(STAGES, 2, rows, D)
        mine = lax.dynamic_index_in_dim(parts, core, 1, keepdims=False)
        other = lax.dynamic_index_in_dim(parts, 1 - core, 1, keepdims=False)
        return mine, other

    def own_rows(block):
        cut = block.reshape(2, block.shape[0] // 2, block.shape[1])
        mine = lax.dynamic_index_in_dim(cut, core, 0, keepdims=False)
        other = lax.dynamic_index_in_dim(cut, 1 - core, 0, keepdims=False)
        return jnp.stack(by_core(mine, partner(other)))

    hidden_rows = feed_out.shape[0]
    out_blocks = group_blocks(
        place,
        [(hidden, cots, [(0, hidden_rows, 0, 0)])],
        (hidden_rows, 256),
        None,
        "fo" in STAGE_FIRST,
    )
    out_sums = Reduction(order, "fo", out_blocks)
    cots_held = after(cots, out_blocks[1])
    grad_pre = narrow(product_t(order.step("pre", cots_held), w_out) * wide(slope))
    in_sums = Reduction(
        order,
        "fi",
        group_blocks(
            place,
            [(normed2, grad_pre, [(0, 256, 0, 0)])],
            (256, 512),
            None,
            "fi" in STAGE_FIRST,
        ),
    )

    part2 = product_t(grad_pre, w_in)
    grad_norm2 = order.step("norm2", pair_sum(part2))
    grad_after_cross = wide(cots) + normal_back(unit2, scale2, gains[2], grad_norm2)
    branch2 = narrow(grad_after_cross)
    grad_cross = narrow(product_t(branch2, w_cross))
    grad_query, grad_key, grad_value = attend_back_pair(
        text_bias_rows,
        (query, 0),
        (keyval, 0),
        (keyval, 4),
        order.step("cross.back", grad_cross),
        cross,
        cross_levels,
        False,
    )
    part1 = product_t(grad_query, w_query)
    grad_norm1 = order.step("norm1", pair_sum(part1))
    grad_after_self = grad_after_cross + normal_back(unit1, scale1, gains[1], grad_norm1)
    grad_keyval = jnp.concatenate([grad_key, grad_value], 1)
    grad_encoded = narrow(pair_sum(product_t(grad_keyval, w_keyval)))
    grad_encoded_mine = lax.dynamic_slice_in_dim(grad_encoded, core * half, half, 1)
    grad_words = product_t(grad_encoded_mine, w_text).reshape(STAGES, 2, -1, ENC)
    words_mine = lax.dynamic_index_in_dim(grad_words, core, 1, keepdims=False)
    words_other = lax.dynamic_index_in_dim(grad_words, 1 - core, 1, keepdims=False)
    text_result = narrow(words_mine + wide(partner(narrow(words_other))))
    own_words = text_result.shape[1]
    text_result = jnp.pad(text_result, ((0, 0), (0, 16 - own_words), (0, D - ENC)))

    branch1 = narrow(grad_after_self)
    cross_sums = Reduction(
        order,
        "cr",
        group_blocks(
            place,
            [
                (order.step("cr", cross), branch2, [(0, 128, 0, 0)]),
                (normed1, grad_query, [(0, 256, 128, 0)]),
                (words_padded, grad_encoded_mine, [(0, 256, 128, 128)]),
                (encoded, grad_keyval, [(0, 256, 384, 0)]),
            ],
            (640, 256),
        )
    )
    grad_mixed = order.step("attend.back", narrow(product_t(branch1, w_self)))
    grad_qkv = jnp.concatenate(
        attend_back_pair(
            key_bias, (qkv, 0), (qkv, 4), (qkv, 8), grad_mixed, mixed, levels, True
        ),
        1,
    )
    part0 = product_t(order.step("part0", grad_qkv), w_qkv)
    sums = jnp.stack(
        [
            jnp.sum(part0 * unit0, 0),
            jnp.sum(part1 * unit1, 0),
            jnp.sum(part2 * unit2, 0),
            jnp.sum(part0, 0),
            jnp.sum(part1, 0),
            jnp.sum(part2, 0),
            0.5 * jnp.sum(wide(grad_encoded), 0),
            jnp.zeros((D,), jnp.float32),
        ]
    )
    sums = jnp.pad(narrow(sums).reshape(PARTS, 2, D), ((0, 0), (0, 14), (0, 0)))
    late_blocks = group_blocks(
        place,
        [
            (order.step("late", normed0), grad_qkv, [(0, 128, 128, 0), (128, 128, 272, 0)]),
            (mixed, branch1, [(0, 128, 0, 0)]),
        ],
        (416, 384),
        sums,
    )
    order.note("blocks", late_blocks[0])
    norm0_mine, norm0_other = split_rows(order.behind("<scale", part0))
    grad_norm0 = norm0_mine + wide(partner(narrow(norm0_other)))
    unit0_mine, scale0_mine = normalise(wide(order.behind("<scale", frames_mine)))
    after_self_mine, _ = split_rows(order.behind("<scale", grad_after_self))
    grad_inputs = after_self_mine + normal_back(unit0_mine, scale0_mine, gains[0], grad_norm0)
    moved = stage_exchange(
        order.behind("<moved", jnp.concatenate([narrow(grad_inputs), text_result], 1))
    )
    order.note("moved", moved)
    result_mine, result_other = split_rows(product(order.behind("<result", hidden), w_out))
    base_mine, _ = split_rows(after_cross)
    result = stage_exchange(narrow(base_mine + result_mine + wide(partner(narrow(result_other)))))
    order.note("result", result)
    late_sums = Reduction(order, "late", late_blocks)
    longs, shorts = moved[: STAGES // 2], moved[STAGES // 2 :]
    words_at = slice(rows, rows + own_words)

    (feed_out_grad,) = finish(
        place, out_sums.block(), [(feed_out.shape, [(..., 256, lambda part: part * 256)])]
    )

    def interleaved(width):
        return [
            ((side,), width, lambda part, side=side: (2 * part + side) * width)
            for side in range(2)
        ]

    (feed_in_grad,) = finish(
        place, own_rows(in_sums.block()), [(feed_in.shape, interleaved(512))]
    )
    cross_block, shard = cross_sums.block(), D // 8
    sides = own_rows(
        cross_block[shard:].reshape(2, 2, shard, 256).transpose(1, 0, 2, 3).reshape(4 * shard, 256)
    )
    cross_block = jnp.concatenate([cross_block[:shard], sides.reshape(4 * shard, 256)], 0)

    def rows_at(first, count=shard, lanes=slice(None)):
        return (slice(first, first + count), lanes)

    cross_out_grad, cross_query_grad, text_proj_grad, cross_keyval_grad = finish(
        place,
        cross_block,
        [
            (cross_out.shape, [(rows_at(0), 256, lambda part: part * 256)]),
            (
                cross_query.shape,
                [
                    (
                        rows_at((1 + 2 * side) * shard, shard, slice(0, 128)),
                        128,
                        lambda part, side=side: (2 * part + side) * 128,
                    )
                    for side in range(2)
                ],
            ),
            (
                text_proj.shape,
                [
                    (
                        rows_at((1 + 2 * side) * shard, text_rows, slice(128, 256)),
                        128,
                        lambda part, side=side: side * half + part * 128,
                    )
                    for side in range(2)
                ],
            ),
            (
                cross_keyval.shape,
                [
                    (
                        rows_at((2 + 2 * side) * shard, shard, slice(128 * j, 128 * j + 128)),
                        128,
                        lambda part, side=side, j=j: (2 * (2 * part + j) + side) * 128,
                    )
                    for side in range(2)
                    for j in range(2)
                ],
            ),
        ],
    )
    late_block = late_sums.block()
    sides = own_rows(late_block[shard:]).reshape(2 * (shard + 16), 384)
    self_out_grad, qkv_grad, sums = finish(
        place,
        jnp.concatenate([late_block[:shard], sides], 0),
        [
            (self_out.shape, [(rows_at(0, shard, slice(0, 256)), 256, lambda part: part * 256)]),
            (
                qkv_weight.shape,
                [
                    (
                        rows_at(
                            shard + side * (shard + 16), shard, slice(128 * j, 128 * j + 128)
                        ),
                        128,
                        lambda part, side=side, j=j: (2 * (3 * part + j) + side) * 128,
                    )
                    for side in range(2)
                    for j in range(3)
                ],
            ),
        ],
        (2 * shard, 3 * shard + 16),
    )
    sums = sums[:, :2].reshape(8, shard)
    return (
        result[: STAGES // 2],
        result[STAGES // 2 :, :short_rows],
        wide(longs[:, :rows]),
        wide(shorts[:, :short_rows]),
        wide(longs[:, words_at, :ENC]),
        wide(shorts[:, words_at, :ENC]),
        qkv_grad,
        self_out_grad,
        cross_query_grad,
        cross_keyval_grad,
        cross_out_grad,
        text_proj_grad,
        sums[6],
        feed_in_grad,
        feed_out_grad,
        sums[0:3],
        sums[3:6],
    )


def solution(mesh):
    return jax.shard_map(
        on_item_device if fits_item_plan(mesh) else on_device,
        mesh=mesh,
        in_specs=(
            P("dp", "seq", None),
            P("dp", "seq", None),
            P("dp", None, None),
            P("dp", None, None),
            P("dp"),
            P("dp"),
            P(None, "dp"),
            P("seq", None),
            P("seq", None),
            P("seq", None),
            P("seq", None),
            P("seq", None),
            P("seq", None),
            P("seq"),
            P("seq", None),
            P("seq", None),
            P(None, "seq"),
            P(None, "seq"),
            P("dp", "seq", None),
            P("dp", "seq", None),
        ),
        out_specs=(
            P("dp", "seq", None),
            P("dp", "seq", None),
            P("dp", "seq", None),
            P("dp", "seq", None),
            P("dp", "seq", None),
            P("dp", "seq", None),
            P("seq", None),
            P("seq", None),
            P("seq", None),
            P("seq", None),
            P("seq", None),
            P("seq", None),
            P("seq"),
            P("seq", None),
            P("seq", None),
            P(None, "seq"),
            P(None, "seq"),
        ),
        check_vma=False,
    )
```

```python
from functools import partial

import jax
import jax.numpy as jnp
from jax import lax
from jax.experimental import pallas as pl
from jax.experimental.pallas import tpu as pltpu
from jax.sharding import PartitionSpec as P

D = 1024
HEADS = 16
ENC = 768
TEXT = 64


masked_value = -1e30
norm_eps = 1e-05


def layer_norm(values, gain_row, bias_row):
    average = jnp.mean(values, -1, keepdims=True)
    centred = values - average
    spread = jnp.mean(centred * centred, -1, keepdims=True)
    return centred * lax.rsqrt(spread + norm_eps) * gain_row + bias_row


def norm_back(values, gain_row, bias_row, incoming):
    _, pullback = jax.vjp(layer_norm, values, gain_row, bias_row)
    return pullback(incoming)


def product(left, right):
    return jnp.dot(left, right, preferred_element_type=jnp.float32)


def product_t(left, right):
    return lax.dot_general(
        left, right, (((left.ndim - 1,), (1,)), ((), ())), preferred_element_type=jnp.float32
    )


def weight_grad(left, right):
    return lax.dot_general(
        left, right, (((0,), (0,)), ((), ())), preferred_element_type=jnp.float32
    )


def head_view(packed, head_dim):
    return packed.reshape(packed.shape[0], packed.shape[1], -1, head_dim)


def flatten_heads(tensor):
    return tensor.reshape(tensor.shape[0], tensor.shape[1], -1).astype(jnp.bfloat16)


def softmax_weights(query, keys, mask, score_scale):
    scores = (
        jnp.einsum("iqhd,ikhd->ihqk", query, keys, preferred_element_type=jnp.float32) * score_scale
    )
    scores = jnp.where(mask, scores, masked_value)
    row_max = jnp.max(scores, -1, keepdims=True)
    raised = jnp.exp(scores - row_max)
    return raised / jnp.sum(raised, -1, keepdims=True)


def attend_forward(query, keys, values, mask, score_scale):
    weights = softmax_weights(query, keys, mask, score_scale).astype(jnp.bfloat16)
    mixed = jnp.einsum("ihqk,ikhd->iqhd", weights, values, preferred_element_type=jnp.float32)
    return flatten_heads(mixed)


def attend_backward(query, keys, values, mask, score_scale, grad_out):
    probs = softmax_weights(query, keys, mask, score_scale)
    grad_values = jnp.einsum(
        "ihqk,iqhd->ikhd", probs.astype(jnp.bfloat16), grad_out, preferred_element_type=jnp.float32
    )
    grad_probs = jnp.einsum("iqhd,ikhd->ihqk", grad_out, values, preferred_element_type=jnp.float32)
    centre = jnp.sum(probs * grad_probs, -1, keepdims=True)
    grad_scores = (probs * (grad_probs - centre)).astype(jnp.bfloat16)
    grad_query = (
        jnp.einsum("ihqk,ikhd->iqhd", grad_scores, keys, preferred_element_type=jnp.float32)
        * score_scale
    )
    grad_keys = (
        jnp.einsum("ihqk,iqhd->ikhd", grad_scores, query, preferred_element_type=jnp.float32)
        * score_scale
    )
    return (flatten_heads(grad_query), flatten_heads(grad_keys), flatten_heads(grad_values))


def on_device(
    long_frames,
    short_frames,
    long_text,
    short_text,
    long_lengths,
    short_lengths,
    text_lengths,
    qkv_weight,
    self_out,
    cross_query,
    cross_keyval,
    cross_out,
    text_proj,
    text_bias,
    feed_in,
    feed_out,
    norm_gains,
    norm_shifts,
    long_cot,
    short_cot,
):
    w_qkv, w_self, w_query, w_keyval, w_cross, w_text, b_text, w_in, w_out, gains, shifts = (
        lax.all_gather(qkv_weight, "seq", axis=0, tiled=True),
        lax.all_gather(self_out, "seq", axis=0, tiled=True),
        lax.all_gather(cross_query, "seq", axis=0, tiled=True),
        lax.all_gather(cross_keyval, "seq", axis=0, tiled=True),
        lax.all_gather(cross_out, "seq", axis=0, tiled=True),
        lax.all_gather(text_proj, "seq", axis=0, tiled=True),
        lax.all_gather(text_bias, "seq", axis=0, tiled=True),
        lax.all_gather(feed_in, "seq", axis=0, tiled=True),
        lax.all_gather(feed_out, "seq", axis=0, tiled=True),
        lax.all_gather(norm_gains, "seq", axis=1, tiled=True),
        lax.all_gather(norm_shifts, "seq", axis=1, tiled=True),
    )
    seq_count = lax.axis_size("seq")
    seq_rank = lax.axis_index("seq")
    head_dim = D // HEADS
    head_width = D // seq_count
    score_scale = head_dim ** (-0.5)
    item_count, long_rows, _ = long_frames.shape
    short_rows = short_frames.shape[1]
    long_total = item_count * long_rows
    long_len = long_rows * seq_count
    short_len = short_rows * seq_count

    def to_items(joined):
        last_dim = joined.shape[-1]
        return (
            joined[:long_total].reshape(item_count, long_rows, last_dim),
            joined[long_total:].reshape(item_count, short_rows, last_dim),
        )

    def to_rows(long_part, short_part):
        return jnp.concatenate(
            [
                long_part.reshape(long_part.shape[0] * long_part.shape[1], -1),
                short_part.reshape(short_part.shape[0] * short_part.shape[1], -1),
            ],
            0,
        )

    def self_mask(lengths, full):
        places = jnp.arange(full)
        causal = places[:, None] >= places[None, :]
        return causal[None, None] & (places[None, None, None, :] < lengths[:, None, None, None])

    def text_mask(lengths):
        places = jnp.arange(TEXT)
        return (places[None, :] < lengths[:, None])[:, None, None, :]

    def split_three(packed):
        return (
            head_view(packed[:, :, 0], head_dim),
            head_view(packed[:, :, 1], head_dim),
            head_view(packed[:, :, 2], head_dim),
        )

    masks_self = (self_mask(long_lengths, long_len), self_mask(short_lengths, short_len))
    masks_text = (text_mask(text_lengths[0]), text_mask(text_lengths[1]))
    inputs = to_rows(long_frames, short_frames).astype(jnp.float32)
    normed_self = layer_norm(inputs, gains[0], shifts[0]).astype(jnp.bfloat16)

    def self_heads():
        packed = product(normed_self, w_qkv).astype(jnp.bfloat16)
        long_part, short_part = to_items(packed)
        long_part = long_part.reshape(item_count, long_rows, 3, D)
        short_part = short_part.reshape(item_count, short_rows, 3, D)
        return (
            lax.all_to_all(long_part, "seq", split_axis=3, concat_axis=1, tiled=True),
            lax.all_to_all(short_part, "seq", split_axis=3, concat_axis=1, tiled=True),
        )

    heads_pair = self_heads()
    long_mixed = attend_forward(*split_three(heads_pair[0]), masks_self[0], score_scale)
    short_mixed = attend_forward(*split_three(heads_pair[1]), masks_self[1], score_scale)
    long_back, short_back = (
        lax.all_to_all(long_mixed, "seq", split_axis=1, concat_axis=2, tiled=True),
        lax.all_to_all(short_mixed, "seq", split_axis=1, concat_axis=2, tiled=True),
    )
    self_rows = to_rows(long_back, short_back)
    after_self = inputs + product(self_rows, w_self)
    normed_cross = layer_norm(after_self, gains[1], shifts[1]).astype(jnp.bfloat16)
    long_query, short_query = to_items(product(normed_cross, w_query).astype(jnp.bfloat16))
    query_heads = (
        lax.all_to_all(long_query, "seq", split_axis=2, concat_axis=1, tiled=True),
        lax.all_to_all(short_query, "seq", split_axis=2, concat_axis=1, tiled=True),
    )
    key_cols = lax.dynamic_slice_in_dim(w_keyval, seq_rank * head_width, head_width, 1)
    value_cols = lax.dynamic_slice_in_dim(w_keyval, D + seq_rank * head_width, head_width, 1)
    texts = (long_text, short_text)
    encoded = tuple(((product(words, w_text) + b_text).astype(jnp.bfloat16) for words in texts))
    text_keys = tuple((product(enc_rows, key_cols).astype(jnp.bfloat16) for enc_rows in encoded))
    text_values = tuple(
        (product(enc_rows, value_cols).astype(jnp.bfloat16) for enc_rows in encoded)
    )
    cross_long = attend_forward(
        head_view(query_heads[0], head_dim),
        head_view(text_keys[0], head_dim),
        head_view(text_values[0], head_dim),
        masks_text[0],
        score_scale,
    )
    cross_short = attend_forward(
        head_view(query_heads[1], head_dim),
        head_view(text_keys[1], head_dim),
        head_view(text_values[1], head_dim),
        masks_text[1],
        score_scale,
    )
    cross_back_long, cross_back_short = (
        lax.all_to_all(cross_long, "seq", split_axis=1, concat_axis=2, tiled=True),
        lax.all_to_all(cross_short, "seq", split_axis=1, concat_axis=2, tiled=True),
    )
    cross_rows = to_rows(cross_back_long, cross_back_short)
    after_cross = after_self + product(cross_rows, w_cross)
    normed_feed = layer_norm(after_cross, gains[2], shifts[2]).astype(jnp.bfloat16)
    pre_act = product(normed_feed, w_in)
    hidden = jax.nn.gelu(pre_act, approximate=False).astype(jnp.bfloat16)
    result = after_cross + product(hidden, w_out)
    grad_rows = to_rows(long_cot, short_cot)
    feed_out_grad = weight_grad(hidden, grad_rows)
    _, gelu_pull = jax.vjp(partial(jax.nn.gelu, approximate=False), pre_act)
    grad_pre = gelu_pull(product_t(grad_rows, w_out))[0].astype(jnp.bfloat16)
    feed_in_grad = weight_grad(normed_feed, grad_pre)
    grad_cross_in, gain_two, shift_two = norm_back(
        after_cross, gains[2], shifts[2], product_t(grad_pre, w_in)
    )
    grad_after_cross = grad_rows.astype(jnp.float32) + grad_cross_in
    cross_branch = grad_after_cross.astype(jnp.bfloat16)
    cross_out_grad = weight_grad(cross_rows, cross_branch)
    long_dco, short_dco = to_items(product_t(cross_branch, w_cross).astype(jnp.bfloat16))
    grad_heads = (
        lax.all_to_all(long_dco, "seq", split_axis=2, concat_axis=1, tiled=True),
        lax.all_to_all(short_dco, "seq", split_axis=2, concat_axis=1, tiled=True),
    )
    cross_parts = tuple(
        (
            attend_backward(
                head_view(query_heads[bucket], head_dim),
                head_view(text_keys[bucket], head_dim),
                head_view(text_values[bucket], head_dim),
                masks_text[bucket],
                score_scale,
                head_view(grad_heads[bucket], head_dim),
            )
            for bucket in range(2)
        )
    )
    long_dq, short_dq = (
        lax.all_to_all(cross_parts[0][0], "seq", split_axis=1, concat_axis=2, tiled=True),
        lax.all_to_all(cross_parts[1][0], "seq", split_axis=1, concat_axis=2, tiled=True),
    )
    query_rows = to_rows(long_dq, short_dq)
    cross_query_grad = weight_grad(normed_cross, query_rows)
    grad_self_in, gain_one, shift_one = norm_back(
        after_self, gains[1], shifts[1], product_t(query_rows, w_query)
    )
    grad_after_self = grad_after_cross + grad_self_in
    key_grad = jnp.zeros((D, head_width), jnp.float32)
    value_grad = jnp.zeros((D, head_width), jnp.float32)
    for bucket in range(2):
        key_grad = key_grad + jnp.einsum(
            "itd,itw->dw",
            encoded[bucket],
            cross_parts[bucket][1],
            preferred_element_type=jnp.float32,
        )
        value_grad = value_grad + jnp.einsum(
            "itd,itw->dw",
            encoded[bucket],
            cross_parts[bucket][2],
            preferred_element_type=jnp.float32,
        )
    keyval_grad = jnp.zeros((D, 2 * D), jnp.float32)
    keyval_grad = lax.dynamic_update_slice_in_dim(keyval_grad, key_grad, seq_rank * head_width, 1)
    keyval_grad = lax.dynamic_update_slice_in_dim(
        keyval_grad, value_grad, D + seq_rank * head_width, 1
    )
    enc_long = product_t(cross_parts[0][1], key_cols) + product_t(cross_parts[0][2], value_cols)
    enc_short = product_t(cross_parts[1][1], key_cols) + product_t(cross_parts[1][2], value_cols)
    summed_long, summed_short = (
        lax.psum_scatter(
            enc_long.astype(jnp.bfloat16), "seq", scatter_dimension=1, tiled=True
        ).astype(jnp.float32),
        lax.psum_scatter(
            enc_short.astype(jnp.bfloat16), "seq", scatter_dimension=1, tiled=True
        ).astype(jnp.float32),
    )
    enc_grads = (summed_long.astype(jnp.bfloat16), summed_short.astype(jnp.bfloat16))
    text_rows = TEXT // seq_count
    own_text = tuple(
        (lax.dynamic_slice_in_dim(words, seq_rank * text_rows, text_rows, 1) for words in texts)
    )
    text_grads = tuple((product_t(enc_grad, w_text) for enc_grad in enc_grads))
    text_proj_grad = jnp.zeros((ENC, D), jnp.float32)
    text_bias_grad = jnp.zeros((D,), jnp.float32)
    for bucket in range(2):
        text_proj_grad = text_proj_grad + jnp.einsum(
            "ite,itd->ed", own_text[bucket], enc_grads[bucket], preferred_element_type=jnp.float32
        )
        text_bias_grad = text_bias_grad + jnp.sum(enc_grads[bucket].astype(jnp.float32), (0, 1))
    self_branch = grad_after_self.astype(jnp.bfloat16)
    self_out_grad = weight_grad(self_rows, self_branch)
    long_do, short_do = to_items(product_t(self_branch, w_self).astype(jnp.bfloat16))
    out_heads = (
        lax.all_to_all(long_do, "seq", split_axis=2, concat_axis=1, tiled=True),
        lax.all_to_all(short_do, "seq", split_axis=2, concat_axis=1, tiled=True),
    )
    kept_heads = self_heads()
    self_parts = tuple(
        (
            attend_backward(
                *split_three(kept_heads[bucket]),
                masks_self[bucket],
                score_scale,
                head_view(out_heads[bucket], head_dim)
            )
            for bucket in range(2)
        )
    )
    stacked_long = jnp.stack(self_parts[0], 2)
    stacked_short = jnp.stack(self_parts[1], 2)
    long_qkv, short_qkv = (
        lax.all_to_all(stacked_long, "seq", split_axis=1, concat_axis=3, tiled=True),
        lax.all_to_all(stacked_short, "seq", split_axis=1, concat_axis=3, tiled=True),
    )
    qkv_rows = to_rows(long_qkv, short_qkv)
    qkv_grad = weight_grad(normed_self, qkv_rows)
    grad_first, gain_zero, shift_zero = norm_back(
        inputs, gains[0], shifts[0], product_t(qkv_rows, w_qkv)
    )
    input_grad = grad_after_self + grad_first
    grads = (
        qkv_grad,
        self_out_grad,
        cross_query_grad,
        keyval_grad,
        cross_out_grad,
        text_proj_grad,
        text_bias_grad,
        feed_in_grad,
        feed_out_grad,
        jnp.stack([gain_zero, gain_one, gain_two]),
        jnp.stack([shift_zero, shift_one, shift_two]),
    )
    shares = (
        lax.psum_scatter(
            grads[0].astype(jnp.bfloat16), "seq", scatter_dimension=0, tiled=True
        ).astype(jnp.float32),
        lax.psum_scatter(
            grads[1].astype(jnp.bfloat16), "seq", scatter_dimension=0, tiled=True
        ).astype(jnp.float32),
        lax.psum_scatter(
            grads[2].astype(jnp.bfloat16), "seq", scatter_dimension=0, tiled=True
        ).astype(jnp.float32),
        lax.psum_scatter(
            grads[3].astype(jnp.bfloat16), "seq", scatter_dimension=0, tiled=True
        ).astype(jnp.float32),
        lax.psum_scatter(
            grads[4].astype(jnp.bfloat16), "seq", scatter_dimension=0, tiled=True
        ).astype(jnp.float32),
        lax.psum_scatter(
            grads[5].astype(jnp.bfloat16), "seq", scatter_dimension=0, tiled=True
        ).astype(jnp.float32),
        lax.psum_scatter(
            grads[6].astype(jnp.bfloat16), "seq", scatter_dimension=0, tiled=True
        ).astype(jnp.float32),
        lax.psum_scatter(
            grads[7].astype(jnp.bfloat16), "seq", scatter_dimension=0, tiled=True
        ).astype(jnp.float32),
        lax.psum_scatter(
            grads[8].astype(jnp.bfloat16), "seq", scatter_dimension=0, tiled=True
        ).astype(jnp.float32),
        lax.psum_scatter(grads[9], "seq", scatter_dimension=1, tiled=True).astype(jnp.float32),
        lax.psum_scatter(grads[10], "seq", scatter_dimension=1, tiled=True).astype(jnp.float32),
    )
    totals = (
        lax.psum(shares[0].astype(jnp.bfloat16), "dp").astype(jnp.float32),
        lax.psum(shares[1].astype(jnp.bfloat16), "dp").astype(jnp.float32),
        lax.psum(shares[2].astype(jnp.bfloat16), "dp").astype(jnp.float32),
        lax.psum(shares[3].astype(jnp.bfloat16), "dp").astype(jnp.float32),
        lax.psum(shares[4].astype(jnp.bfloat16), "dp").astype(jnp.float32),
        lax.psum(shares[5].astype(jnp.bfloat16), "dp").astype(jnp.float32),
        lax.psum(shares[6].astype(jnp.bfloat16), "dp").astype(jnp.float32),
        lax.psum(shares[7].astype(jnp.bfloat16), "dp").astype(jnp.float32),
        lax.psum(shares[8].astype(jnp.bfloat16), "dp").astype(jnp.float32),
        lax.psum(shares[9].astype(jnp.bfloat16), "dp").astype(jnp.float32),
        lax.psum(shares[10].astype(jnp.bfloat16), "dp").astype(jnp.float32),
    )
    long_output, short_output = to_items(result.astype(jnp.bfloat16))
    long_input_grad, short_input_grad = to_items(input_grad)
    return (
        long_output,
        short_output,
        long_input_grad,
        short_input_grad,
        text_grads[0],
        text_grads[1],
        totals[0],
        totals[1],
        totals[2],
        totals[3],
        totals[4],
        totals[5],
        totals[6],
        totals[7],
        totals[8],
        totals[9],
        totals[10],
    )


STAGES = 4
PARTS = 4
ALL_AXES = ("dp", "seq")


def fits_item_plan(mesh):
    return dict(mesh.shape) == {"dp": PARTS, "seq": 2 * STAGES}


def partner(values):
    return lax.ppermute(values, "seq", [(rank, rank ^ 1) for rank in range(2 * STAGES)])


def stage_shift(values, hop):
    count = 2 * STAGES
    pairs = [(rank, (rank + 2 * hop) % count) for rank in range(count)]
    return lax.ppermute(values, "seq", pairs)


def across(values, slot):
    pairs = []
    for group in range(PARTS):
        for rank in range(2 * STAGES):
            flip = (0, 1 + rank % 2, 2 - rank % 2, 3)[slot]
            pairs.append((group * 2 * STAGES + rank, (group ^ flip) * 2 * STAGES + rank))
    return lax.ppermute(values, ALL_AXES, pairs)


def stage_exchange(blocks):
    groups = [[2 * stage + core for stage in range(STAGES)] for core in range(2)]
    return lax.all_to_all(
        blocks, "seq", split_axis=0, concat_axis=0, axis_index_groups=groups, tiled=True
    )


def part_of(group, core, slot):
    flips = (0, 1 + core, 2 - core, 3)
    return lax.bitwise_xor(group, flips[slot])


def kernel_params(limit=40 << 20):
    return pltpu.CompilerParams(vmem_limit_bytes=limit)


RINGS = ('mid', 'qkv')
STAGE_FIRST = ('fo',)
ORDER = {'in<hops': ['frames'], 'out<hops': ['mid.third'], '<cots': ['out.hops'], '<frames': ['mid.hops', 'qkv.third', 'w'], 'mid<hops': ['qkv.hops'], 'in<cross': ['mid.third'], 'out<cross': ['in.third'], 'in.cross': 'self.sum', 'cots': 'feed', 'in.third': 'cross', '<result': ['blocks'], 'fo.moving': 'late', 'fi.moving': 'late.got', 'cr.send': 'late.got', 'result': 'late.got', 'cr.moving': 'late.got', 'words': 'query'}
VMEM_SPEC = pl.BlockSpec(memory_space=pltpu.VMEM)
SMEM_SPEC = pl.BlockSpec(memory_space=pltpu.SMEM)
ANY_SPEC = pl.BlockSpec(memory_space=pl.ANY)
HBM_SPEC = pl.BlockSpec(memory_space=pltpu.HBM)


LANES = 512


def after(values, *others):
    return lax.optimization_barrier((values, *others))[0]


def run_moves(moves, sems):
    started = []
    for number, (source, target) in enumerate(moves):
        move = pltpu.make_async_copy(source, target, sems.at[number])
        move.start()
        started.append(move)
    for move in started:
        move.wait()


def move_call(place, operands, out_shapes, plan, raw=0):
    n, m = len(operands), len(out_shapes)

    class Blank:
        @property
        def at(self):
            return self

        def __getitem__(self, _):
            return self

    count = len(plan((0, 0, 0), [Blank()] * n, [Blank()] * m))

    def kernel(place_ref, *refs):
        spots = (place_ref[0], place_ref[1], place_ref[2])
        run_moves(plan(spots, refs[:n], refs[n : n + m]), refs[n + m])

    return pl.pallas_call(
        kernel,
        out_shape=[jax.ShapeDtypeStruct(shape, jnp.bfloat16) for shape in out_shapes],
        in_specs=[SMEM_SPEC] + [ANY_SPEC] * (n - raw) + [HBM_SPEC] * raw,
        out_specs=[ANY_SPEC] * m,
        scratch_shapes=[pltpu.SemaphoreType.DMA((count,))],
        compiler_params=kernel_params(16 << 20),
    )(place, *operands)


def aligned(value, unit):
    return value if isinstance(value, int) else pl.multiple_of(value, unit)


class Split:
    def __init__(self, matrix, width, halves=False):
        self.matrix, self.width, self.halves = matrix, width, halves
        self.rows = matrix.shape[0]
        self.count = matrix.shape[1] // 2 // LANES
        self.part_rows = self.rows * 2 // PARTS
        self.shape = (self.rows * 2 * STAGES, matrix.shape[1] // 2)


class Whole:
    def __init__(self, matrix):
        self.matrix = matrix
        self.rows = matrix.shape[0]
        self.count = matrix.shape[1] // LANES
        self.part_rows = self.rows // PARTS
        self.shape = (self.rows * STAGES, matrix.shape[1])


def cut_columns(place, splits):
    total = 0
    for entry in splits:
        entry.start = total
        total += entry.rows * entry.count

    def plan(spots, refs, outs):
        moves = []
        for ref, entry in zip(refs, splits):
            width = entry.width
            for j in range(entry.count * LANES // width):
                target = (
                    pl.ds(entry.start + j * width // LANES * entry.rows, entry.rows),
                    pl.ds(j * width % LANES, width),
                )
                for side, out in enumerate(outs):
                    core = spots[2] if side == 0 else 1 - spots[2]
                    column = core * LANES if entry.halves else (2 * j + core) * width
                    moves.append((ref.at[:, pl.ds(aligned(column, 128), width)], out.at[target]))
        return moves

    mine, others = move_call(
        place,
        [entry.matrix for entry in splits],
        [(total, LANES)] * 2,
        plan,
        len(splits),
    )
    return mine, partner(others)


def pack_parts(place, entries, packed):
    wholes = [entry for entry in entries if isinstance(entry, Whole)]
    total = 0
    for entry in entries:
        entry.offset = total
        total += entry.part_rows * entry.count
    operands = list(packed or ()) + [entry.matrix for entry in wholes]
    first = len(operands) - len(wholes)

    def sources(spots, refs, flipped):
        moves = []
        for entry in entries:
            size = entry.part_rows
            for j in range(entry.count):
                if isinstance(entry, Whole):
                    ref = refs[first + wholes.index(entry)]
                    row = aligned(spots[1] * size, size)
                    source = ref.at[pl.ds(row, size), pl.ds(j * LANES, LANES)]
                else:
                    row = entry.start + j * entry.rows + (spots[1] & 1) * size
                    source = refs[1 if flipped else 0].at[pl.ds(aligned(row, 16), size)]
                moves.append((source, (pl.ds(entry.offset + j * size, size),)))
        return moves

    n = len(operands)
    count = sum(entry.count for entry in entries)

    def kernel(place_ref, *refs):
        spots = (place_ref[0], place_ref[1], place_ref[2])
        out, sems = refs[n], refs[n + 1]
        other = lax.bitwise_xor(lax.shift_right_logical(spots[1], 1), spots[2])
        for flipped in range(2):

            @pl.when(other == flipped)
            def _():
                moves = sources(spots, refs, flipped == 1)
                run_moves([(source, out.at[target]) for source, target in moves], sems)

    return pl.pallas_call(
        kernel,
        out_shape=jax.ShapeDtypeStruct((total, LANES), jnp.bfloat16),
        in_specs=[SMEM_SPEC] + [ANY_SPEC] * first + [HBM_SPEC] * len(wholes),
        out_specs=ANY_SPEC,
        scratch_shapes=[pltpu.SemaphoreType.DMA((count,))],
        compiler_params=kernel_params(16 << 20),
    )(place, *operands)


def stage_hops(mine, ring):
    hops = []
    for hop in range(1, STAGES):
        hops.append(stage_shift(hops[-1] if ring and hops else mine, 1 if ring else hop))
    return hops


def assemble(place, entries, packed, shared):
    wholes = [entry for entry in entries if isinstance(entry, Whole)]
    operands = list(shared) + list(packed or ()) + [entry.matrix for entry in wholes]
    first = len(operands) - len(wholes)

    def plan(spots, refs, outs):
        stage, group, core = spots
        moves = []
        for out, entry in zip(outs, entries):
            size = entry.part_rows
            rows = size * PARTS
            for j in range(entry.count):
                lanes = pl.ds(j * LANES, LANES)
                if isinstance(entry, Whole):
                    moves.append(
                        (
                            refs[first + wholes.index(entry)].at[:, lanes],
                            out.at[pl.ds(aligned(stage * rows, rows), rows), lanes],
                        )
                    )
                else:
                    for side in range(2):
                        row = stage * rows + (core if side == 0 else 1 - core) * entry.rows
                        moves.append(
                            (
                                refs[4 + side].at[
                                    pl.ds(entry.start + j * entry.rows, entry.rows)
                                ],
                                out.at[pl.ds(aligned(row, entry.rows), entry.rows), lanes],
                            )
                        )
                for hop in range(1, STAGES):
                    source_stage = (stage + STAGES - hop) & (STAGES - 1)
                    for slot in range(PARTS):
                        part = group ^ (0, 1 + core, 2 - core, 3)[slot]
                        row = aligned(source_stage * rows + part * size, size)
                        moves.append(
                            (
                                refs[slot].at[hop - 1, pl.ds(entry.offset + j * size, size)],
                                out.at[pl.ds(row, size), lanes],
                            )
                        )
        return moves

    return move_call(place, operands, [entry.shape for entry in entries], plan, len(wholes))


def group_blocks(place, pairs, shape, sums=None, by_hop=False):
    n = len(pairs)
    out_shapes = [(PARTS, *shape)] * STAGES if by_hop else [(2, STAGES, *shape)] * 2
    outs = len(out_shapes)

    def kernel(place_ref, *refs):
        stage, group, core = place_ref[0], place_ref[1], place_ref[2]
        out_refs = refs[-outs:]
        for to_stage in range(STAGES):
            hop = (stage + STAGES - to_stage) & (STAGES - 1)
            results = []
            for number, (left, right, _) in enumerate(pairs):
                rows = left.shape[1] // STAGES
                results.append(
                    lax.dot_general(
                        refs[2 * number][:, to_stage * rows : (to_stage + 1) * rows],
                        refs[2 * number + 1][...],
                        (((0,), (0,)), ((), ())),
                        preferred_element_type=jnp.float32,
                    ).astype(jnp.bfloat16)
                )
            for part in range(PARTS):
                apart = group ^ part
                slot = jnp.where((core == 1) & (apart != 0) & (apart != 3), 3 - apart, apart)
                slot = jnp.asarray(slot, jnp.int32)

                def put(out_ref, *index):
                    for result, (left, right, moves) in zip(results, pairs):
                        columns = right.shape[1] // PARTS
                        for first, count, row, lane, *cut in moves:
                            start, size = cut or (0, columns)
                            spot = (slice(row, row + count), slice(lane, lane + size))
                            start += part * columns
                            out_ref[(*index, *spot)] = result[
                                first : first + count, start : start + size
                            ]
                    if sums is not None:
                        for side in range(2):
                            row = shape[0] - 16 - (1 - side) * 144
                            lane = 256 * to_stage + 128 * side
                            out_ref[(*index, slice(row, row + 16), slice(0, 128))] = refs[2 * n][
                                part, :, lane : lane + 128
                            ]
                            out_ref[(*index, slice(row, row + 16), slice(128, None))] = jnp.zeros(
                                (16, shape[1] - 128), jnp.bfloat16
                            )

                if by_hop:
                    for number in range(STAGES):

                        @pl.when(hop == number)
                        def _():
                            put(out_refs[number], slot)

                else:

                    @pl.when(slot >= 2)
                    def _():
                        put(out_refs[0], slot - 2, hop)

                    @pl.when(slot < 2)
                    def _():
                        put(out_refs[1], slot, hop)

    operands = [array for left, right, _ in pairs for array in (left, right)]
    if sums is not None:
        operands.append(sums)
    return pl.pallas_call(
        kernel,
        out_shape=[jax.ShapeDtypeStruct(one, jnp.bfloat16) for one in out_shapes],
        in_specs=[SMEM_SPEC] + [VMEM_SPEC] * len(operands),
        out_specs=[VMEM_SPEC] * outs,
        compiler_params=kernel_params(48 << 20),
    )(place, *operands)


def wide(values):
    return values.astype(jnp.float32)


def narrow(values):
    return values.astype(jnp.bfloat16)


class Order:
    def __init__(self):
        self.results = {}

    def note(self, name, *values):
        self.results[name] = values
        return values[0] if len(values) == 1 else values

    def step(self, name, value):
        waits = [
            value_of
            for key, values in self.results.items()
            if ORDER.get(key) == name
            for value_of in values
        ]
        return after(value, *waits) if waits else value

    def behind(self, name, value):
        waits = [
            one for key in ORDER.get(name, ()) if key in self.results for one in self.results[key]
        ]
        return after(value, *waits) if waits else value


class Reduction:
    def __init__(self, order, name, blocks):
        if name in STAGE_FIRST:
            self.stage_first(order, name, blocks)
            return
        far, near = blocks
        got = order.step(name + ".got", across(far, 2))
        self.send = order.note(name + ".send", narrow(wide(near[1]) + wide(got[1])))
        other = order.step(name + ".other", across(self.send, 1))
        total = [
            wide(near[0, hop]) + wide(got[0, hop]) + wide(other[hop]) for hop in range(STAGES)
        ]
        self.moving = order.note(
            name + ".moving", *[narrow(total[hop]) for hop in range(1, STAGES)]
        )
        moved = [stage_shift(self.moving[hop - 1], -hop) for hop in range(1, STAGES)]
        self.parts = [total[0], *moved]


    def stage_first(self, order, name, blocks):
        moving = stage_shift(blocks[1], 1)
        moving = stage_shift(narrow(wide(blocks[2]) + wide(moving)), 1)
        moving = stage_shift(narrow(wide(blocks[3]) + wide(moving)), 1)
        total = wide(blocks[0]) + wide(moving)
        far = order.note(name + ".moving", narrow(total[2:]))
        got = order.step(name + ".got", across(far, 2))
        self.send = order.note(name + ".send", narrow(total[1] + wide(got[1])))
        other = order.step(name + ".other", across(self.send, 1))
        self.parts = [total[0], got[0], other]

    def block(self):
        total, *rest = self.parts
        for part in rest:
            total = total + wide(part)
        return narrow(total)


def finish(place, block, outs, sums=()):
    first, second = across(block, 1), across(block, 2)
    third = across(first, 2)

    def kernel(place_ref, *refs):
        for slot in range(PARTS):
            part = part_of(place_ref[1], place_ref[2], slot)
            held = refs[slot]
            for out_ref, (_, moves) in zip(refs[PARTS:], outs):
                for index, size, start in moves:
                    column = pl.multiple_of(start(part), 128)
                    out_ref[:, pl.ds(column, size)] = held[index].astype(jnp.float32)
            if sums:
                first_sums, second_sums = (
                    held[row : row + 16, 0:128].astype(jnp.float32) for row in sums
                )
                refs[-1][part] = first_sums + second_sums

    shapes = [shape for shape, _ in outs] + ([(PARTS, 16, 128)] if sums else [])
    return pl.pallas_call(
        kernel,
        out_shape=[jax.ShapeDtypeStruct(shape, jnp.float32) for shape in shapes],
        in_specs=[SMEM_SPEC] + [VMEM_SPEC] * PARTS,
        out_specs=[VMEM_SPEC] * len(shapes),
        compiler_params=kernel_params(),
    )(place, block, first, second, third)


def lanes_of(values):
    return lax.broadcasted_iota(jnp.int32, values.shape, 1)


def of_head(values, head):
    return (lanes_of(values) >= 64) == (head == 1)


def with_terms(values, head, terms):
    out = jnp.where(of_head(values, head), values, 0.0)
    for number, term in enumerate(terms):
        out = jnp.where(lanes_of(values) == 64 * (1 - head) + number, term, out)
    return narrow(out)


def in_three(values):
    first = wide(narrow(values))
    second = wide(narrow(values - first))
    return first, second, wide(narrow(values - first - second))


def tiles_of(length, keys, size, causal):
    if not causal:
        return [(0, length, [(0, keys, False)])]
    tiles = []
    for start in range(0, length, size):
        count = min(size, length - start)
        runs = [(0, start, False)] if start else []
        tiles.append((start, count, runs + [(start, count, 2)]))
    return tiles


def causal_scores(scores, first_key, first_query, diagonal):
    if not diagonal:
        return scores
    key = first_key + lax.broadcasted_iota(jnp.int32, scores.shape, 0)
    query = first_query + lax.broadcasted_iota(jnp.int32, scores.shape, 1)
    return jnp.where(key <= query, scores, masked_value)


def attend_kernel(tiles, bias_ref, q_ref, k_ref, v_ref, out_ref, level_ref):
    query = wide(q_ref[...]) * 0.125
    keys, values = wide(k_ref[...]), wide(v_ref[...])
    bias = bias_ref[...]
    queries = [with_terms(query, head, [1.0]) for head in range(2)]
    keyed = [with_terms(keys, head, [bias]) for head in range(2)]
    turned = [
        jnp.transpose(narrow(jnp.where(of_head(values, head), values, 1.0))) for head in range(2)
    ]
    for start, size, runs in tiles:
        mixed, levels = [], []
        for head in range(2):
            scores = [
                causal_scores(
                    product_t(keyed[head][first : first + count], queries[head][start : start + size]),
                    first,
                    start,
                    diagonal,
                )
                for first, count, diagonal in runs
            ]
            top = jnp.max(scores[0], 0, keepdims=True)
            for more in scores[1:]:
                top = jnp.maximum(top, jnp.max(more, 0, keepdims=True))
            summed = None
            for part, (first, count, _) in zip(scores, runs):
                term = product(turned[head][:, first : first + count], narrow(jnp.exp(part - top)))
                summed = term if summed is None else summed + term
            weight = summed[64 * (1 - head) : 64 * (1 - head) + 1]
            mixed.append(summed[64 * head : 64 * head + 64] * (1.0 / weight))
            levels.append(jnp.broadcast_to(top + jnp.log(weight), (64, size)))
        out_ref[start : start + size, :] = narrow(jnp.transpose(jnp.concatenate(mixed, 0)))
        level_ref[start : start + size, :] = jnp.transpose(jnp.concatenate(levels[::-1], 0))


def pair_specs(bias, blocks):
    return [pl.BlockSpec(bias.shape, lambda pair: (0, 0))] + [
        pl.BlockSpec((size, 128), lambda pair, first=first: (0, first + pair))
        for size, first in blocks
    ]


def attend_pair(bias, query, keys, values, causal):
    length, count = query[0].shape[0], keys[0].shape[0]
    tiles = tiles_of(length, count, length, causal)
    return pl.pallas_call(
        partial(attend_kernel, tiles),
        out_shape=[
            jax.ShapeDtypeStruct((length, 512), jnp.bfloat16),
            jax.ShapeDtypeStruct((length, 512), jnp.float32),
        ],
        grid=(4,),
        in_specs=pair_specs(
            bias, [(length, query[1]), (count, keys[1]), (count, values[1])]
        ),
        out_specs=[pl.BlockSpec((length, 128), lambda pair: (0, pair))] * 2,
        compiler_params=kernel_params(),
    )(bias, query[0], keys[0], values[0])


def attend_back_kernel(
    tiles,
    bias_ref,
    q_ref,
    k_ref,
    v_ref,
    do_ref,
    out_ref,
    level_ref,
    dq_ref,
    dk_ref,
    dv_ref,
    key_sum,
    value_sum,
):
    query = wide(q_ref[...]) * 0.125
    keys, values, grad = wide(k_ref[...]), wide(v_ref[...]), wide(do_ref[...])
    bias = bias_ref[...]
    levels = in_three(-level_ref[...])
    centred = grad * wide(out_ref[...])
    plain_query, plain_grad = narrow(query), do_ref[...]
    turned = jnp.transpose(k_ref[...])
    last = tiles[-1][0]
    grads = []
    for head in range(2):
        centre = -jnp.sum(
            jnp.where(of_head(centred, head), centred, 0.0), -1, keepdims=True
        )
        centres = in_three(centre)
        queries = with_terms(query, head, [1.0, *levels])
        keyed = with_terms(keys, head, [bias, 1.0, 1.0, 1.0])
        outs = with_terms(grad, head, centres)
        valued = with_terms(values, head, [1.0, 1.0, 1.0])
        pieces = []
        for start, size, runs in reversed(tiles):
            rows = slice(start, start + size)
            summed = None
            for first, count, diagonal in runs:
                span = slice(first, first + count)
                probs = jnp.exp(
                    causal_scores(product_t(keyed[span], queries[rows]), first, start, diagonal)
                )
                grad_scores = narrow(probs * product_t(valued[span], outs[rows]))
                value_term = product(narrow(probs), plain_grad[rows])
                key_term = product(grad_scores, plain_query[rows])
                term = product(turned[:, span], grad_scores)
                summed = term if summed is None else summed + term
                if start == last:
                    value_sum[head, span] = value_term
                    key_sum[head, span] = key_term
                else:
                    value_sum[head, span] += value_term
                    key_sum[head, span] += key_term
            pieces.append(summed[64 * head : 64 * head + 64] * 0.125)
        grads.append(pieces)
    for (start, size, _), first, second in zip(reversed(tiles), *grads):
        dq_ref[start : start + size, :] = narrow(
            jnp.transpose(jnp.concatenate([first, second], 0))
        )
    of_second = of_head(keys, 1)
    dk_ref[...] = narrow(jnp.where(of_second, key_sum[1], key_sum[0]))
    dv_ref[...] = narrow(jnp.where(of_second, value_sum[1], value_sum[0]))


def attend_back_pair(bias, query, keys, values, grad_out, mixed, levels, causal):
    length, count = query[0].shape[0], keys[0].shape[0]
    tiles = tiles_of(length, count, 384, causal)
    return pl.pallas_call(
        partial(attend_back_kernel, tiles),
        out_shape=[
            jax.ShapeDtypeStruct((size, 512), jnp.bfloat16) for size in (length, count, count)
        ],
        grid=(4,),
        in_specs=pair_specs(
            bias,
            [(length, query[1]), (count, keys[1]), (count, values[1])] + [(length, 0)] * 3,
        ),
        out_specs=[
            pl.BlockSpec((size, 128), lambda pair: (0, pair)) for size in (length, count, count)
        ],
        scratch_shapes=[pltpu.VMEM((2, count, 128), jnp.float32)] * 2,
        compiler_params=kernel_params(),
    )(bias, query[0], keys[0], values[0], grad_out, mixed, levels)


def feed_kernel(rows_ref, weight_ref, hidden_ref, slope_ref):
    pre = product(rows_ref[...], weight_ref[...])
    below = 0.5 * (1.0 + lax.erf(pre * 0.7071067811865476))
    hidden_ref[...] = narrow(pre * below)
    slope_ref[...] = narrow(below + pre * jnp.exp(pre * pre * -0.5) * 0.3989422804014327)


def feed_forward(rows, weight):
    count, width = rows.shape[0], 512
    return pl.pallas_call(
        feed_kernel,
        out_shape=[jax.ShapeDtypeStruct((count, weight.shape[1]), jnp.bfloat16)] * 2,
        grid=(weight.shape[1] // width,),
        in_specs=[
            pl.BlockSpec((count, rows.shape[1]), lambda step: (0, 0)),
            pl.BlockSpec((weight.shape[0], width), lambda step: (0, step)),
        ],
        out_specs=[pl.BlockSpec((count, width), lambda step: (0, step))] * 2,
        compiler_params=kernel_params(),
    )(rows, weight)


def normalise(values):
    centred = values - jnp.mean(values, -1, keepdims=True)
    scale = lax.rsqrt(jnp.mean(centred * centred, -1, keepdims=True) + norm_eps)
    return centred * scale, scale


def normal_back(unit, scale, gain_row, incoming):
    scaled = incoming * gain_row
    mean_one = jnp.mean(scaled, -1, keepdims=True)
    mean_two = jnp.mean(scaled * unit, -1, keepdims=True)
    return scale * (scaled - mean_one - unit * mean_two)


def on_item_device(
    long_frames,
    short_frames,
    long_text,
    short_text,
    long_lengths,
    short_lengths,
    text_lengths,
    qkv_weight,
    self_out,
    cross_query,
    cross_keyval,
    cross_out,
    text_proj,
    text_bias,
    feed_in,
    feed_out,
    norm_gains,
    norm_shifts,
    long_cot,
    short_cot,
):
    rank, group = lax.axis_index("seq"), lax.axis_index("dp")
    stage, core = rank // 2, rank % 2
    place = jnp.stack([stage, group, core]).astype(jnp.int32)
    is_first = core == 0
    rows, short_rows = long_frames.shape[1], short_frames.shape[1]
    length = rows * 2 * STAGES
    text_count = long_text.shape[1]

    def by_core(mine, other):
        return jnp.where(is_first, mine, other), jnp.where(is_first, other, mine)

    def blocks_of(long_part, short_part):
        padded = jnp.pad(short_part, ((0, 0), (0, rows - short_rows), (0, 0)))
        return jnp.concatenate([long_part, padded], 0)

    half = D // 2
    order = Order()
    qkv_entry = [Split(qkv_weight, 128)]
    qkv_packed = cut_columns(place, qkv_entry)
    params = jnp.concatenate([norm_gains, norm_shifts, text_bias[None]], 0)
    params = jnp.pad(params, ((0, 9), (0, D - params.shape[1])))
    frames = jnp.concatenate(
        [blocks_of(long_frames, short_frames), jnp.broadcast_to(params, (STAGES, 16, D))], 1
    )

    def start_group(name, entries, packed, mine=None):
        mine = pack_parts(place, entries, packed) if mine is None else mine
        mine = order.behind(name + "<hops", mine)
        return order.note(name + ".hops", *stage_hops(mine, name in RINGS))

    def cross_plane(name, hops):
        stack = order.behind(name + "<cross", jnp.stack(hops))
        first, second = order.note(name + ".cross", across(stack, 1), across(stack, 2))
        return stack, first, second

    def end_group(name, entries, packed, parts):
        stack, first, second = parts
        third = across(order.behind(name + "<third", after(first, second)), 2)
        order.note(name + ".third", third)
        return assemble(place, entries, packed, [stack, first, second, third])

    def move_frames():
        order.note("frames", stage_exchange(order.behind("<frames", frames)))

    def move_cots():
        order.note(
            "cots", stage_exchange(order.behind("<cots", blocks_of(long_cot, short_cot)))
        )

    qkv_hops = start_group("qkv", qkv_entry, qkv_packed)
    splits = [
        Split(after(cross_query, qkv_hops[0]), 128),
        Split(after(cross_keyval, qkv_hops[0]), 128),
        Split(after(text_proj, qkv_hops[0]), LANES, True),
        Split(after(feed_in, qkv_hops[0]), 512),
    ]
    packed = cut_columns(place, splits)
    middle_entry = [Whole(self_out), *splits[:3], Whole(cross_out)]
    qkv_parts = cross_plane("qkv", qkv_hops)
    middle_hops = start_group("mid", middle_entry, packed)
    (w_qkv,) = end_group("qkv", qkv_entry, qkv_packed, qkv_parts)
    in_group = ("in", [splits[3]], packed)
    out_group = ("out", [Whole(feed_out)], None)
    in_mine, out_mine = pack_parts(place, *in_group[1:]), pack_parts(place, *out_group[1:])
    order.note("w", w_qkv)
    move_frames()
    middle_parts = cross_plane("mid", middle_hops)
    in_hops = start_group(*in_group, in_mine)
    out_hops = start_group(*out_group, out_mine)
    move_cots()

    (frames,) = order.results["frames"]
    frames_mine = frames[:, :rows]
    frames = jnp.stack(by_core(frames, partner(frames)), 1)
    inputs = wide(frames[:, :, :rows].reshape(length, D))
    small = wide(frames[:, :, rows : rows + 7, : D // 8].transpose(2, 0, 1, 3).reshape(7, D))
    gains, shifts, bias = small[0:3], small[3:6], small[6]

    spots = jnp.arange(length)
    real_rows = jnp.where(stage < STAGES // 2, rows, short_rows)
    frame_limit = lax.dynamic_index_in_dim(
        jnp.concatenate([long_lengths, short_lengths]), stage, keepdims=False
    )
    inside = spots % rows < real_rows
    valid = inside & ((spots // rows) * real_rows + spots % rows < frame_limit)
    key_bias = jnp.where(valid, 0.0, masked_value).astype(jnp.float32)[:, None]
    text_limit = lax.dynamic_index_in_dim(
        jnp.concatenate([text_lengths[0], text_lengths[1]]), stage, keepdims=False
    )
    text_bias_rows = jnp.where(jnp.arange(text_count) < text_limit, 0.0, masked_value)
    text_bias_rows = text_bias_rows.astype(jnp.float32)[:, None]
    words = lax.dynamic_index_in_dim(
        jnp.concatenate([long_text, short_text], 0), stage, keepdims=False
    )

    text_rows = ENC // (2 * STAGES)
    words_padded = jnp.pad(
        words.reshape(text_count, 2 * STAGES, text_rows), ((0, 0), (0, 0), (0, 128 - text_rows))
    ).reshape(text_count, D)
    order.note("words", words_padded)

    def pair_sum(part):
        return part + wide(partner(narrow(part)))

    unit0, scale0 = normalise(inputs)
    normed0 = narrow(unit0 * gains[0] + shifts[0])
    qkv = narrow(product(order.step("qkv", normed0), w_qkv))
    mixed, levels = attend_pair(
        key_bias, (order.step("attend", qkv), 0), (qkv, 4), (qkv, 8), True
    )
    order.note("mixed", mixed)
    w_self, w_query, w_keyval, w_text, w_cross = end_group(
        "mid", middle_entry, packed, middle_parts
    )
    in_parts = cross_plane("in", in_hops)
    after_self = inputs + order.step(
        "self.sum", pair_sum(product(order.step("self", mixed), w_self))
    )
    unit1, scale1 = normalise(after_self)
    normed1 = narrow(unit1 * gains[1] + shifts[1])
    query = narrow(product(order.step("query", normed1), w_query))
    bias_mine = lax.dynamic_slice_in_dim(bias, core * half, half)
    encoded = narrow(product(words, w_text) + bias_mine)
    encoded = jnp.concatenate(by_core(encoded, partner(encoded)), 1)
    keyval = narrow(product(encoded, w_keyval))
    cross, cross_levels = attend_pair(
        text_bias_rows, (query, 0), (keyval, 0), (keyval, 4), False
    )
    order.note("cross", cross)
    (w_in,) = end_group(*in_group, in_parts)
    out_parts = cross_plane("out", out_hops)
    after_cross = after_self + order.step(
        "cross.sum", pair_sum(product(order.step("cross", cross), w_cross))
    )
    unit2, scale2 = normalise(after_cross)
    normed2 = narrow(unit2 * gains[2] + shifts[2])
    hidden, slope = feed_forward(order.step("feed", normed2), w_in)
    order.note("hidden", hidden)
    (w_out,) = end_group(*out_group, out_parts)
    (cots,) = order.results["cots"]
    cots = jnp.stack(by_core(cots, partner(cots)), 1).reshape(length, D)

    def split_rows(values):
        parts = values.reshape(STAGES, 2, rows, D)
        mine = lax.dynamic_index_in_dim(parts, core, 1, keepdims=False)
        other = lax.dynamic_index_in_dim(parts, 1 - core, 1, keepdims=False)
        return mine, other

    def own_rows(block):
        cut = block.reshape(2, block.shape[0] // 2, block.shape[1])
        mine = lax.dynamic_index_in_dim(cut, core, 0, keepdims=False)
        other = lax.dynamic_index_in_dim(cut, 1 - core, 0, keepdims=False)
        return jnp.stack(by_core(mine, partner(other)))

    hidden_rows = feed_out.shape[0]
    out_blocks = group_blocks(
        place,
        [(hidden, cots, [(0, hidden_rows, 0, 0)])],
        (hidden_rows, 256),
        None,
        "fo" in STAGE_FIRST,
    )
    out_sums = Reduction(order, "fo", out_blocks)
    cots_held = after(cots, out_blocks[1])
    grad_pre = narrow(product_t(order.step("pre", cots_held), w_out) * wide(slope))
    in_sums = Reduction(
        order,
        "fi",
        group_blocks(
            place,
            [(normed2, grad_pre, [(0, 256, 0, 0)])],
            (256, 512),
            None,
            "fi" in STAGE_FIRST,
        ),
    )

    part2 = product_t(grad_pre, w_in)
    grad_norm2 = order.step("norm2", pair_sum(part2))
    grad_after_cross = wide(cots) + normal_back(unit2, scale2, gains[2], grad_norm2)
    branch2 = narrow(grad_after_cross)
    grad_cross = narrow(product_t(branch2, w_cross))
    grad_query, grad_key, grad_value = attend_back_pair(
        text_bias_rows,
        (query, 0),
        (keyval, 0),
        (keyval, 4),
        order.step("cross.back", grad_cross),
        cross,
        cross_levels,
        False,
    )
    part1 = product_t(grad_query, w_query)
    grad_norm1 = order.step("norm1", pair_sum(part1))
    grad_after_self = grad_after_cross + normal_back(unit1, scale1, gains[1], grad_norm1)
    grad_keyval = jnp.concatenate([grad_key, grad_value], 1)
    grad_encoded = narrow(pair_sum(product_t(grad_keyval, w_keyval)))
    grad_encoded_mine = lax.dynamic_slice_in_dim(grad_encoded, core * half, half, 1)
    grad_words = product_t(grad_encoded_mine, w_text).reshape(STAGES, 2, -1, ENC)
    words_mine = lax.dynamic_index_in_dim(grad_words, core, 1, keepdims=False)
    words_other = lax.dynamic_index_in_dim(grad_words, 1 - core, 1, keepdims=False)
    text_result = narrow(words_mine + wide(partner(narrow(words_other))))
    own_words = text_result.shape[1]
    text_result = jnp.pad(text_result, ((0, 0), (0, 16 - own_words), (0, D - ENC)))

    branch1 = narrow(grad_after_self)
    cross_sums = Reduction(
        order,
        "cr",
        group_blocks(
            place,
            [
                (order.step("cr", cross), branch2, [(0, 128, 0, 0)]),
                (normed1, grad_query, [(0, 256, 128, 0)]),
                (words_padded, grad_encoded_mine, [(0, 256, 128, 128)]),
                (encoded, grad_keyval, [(0, 256, 384, 0)]),
            ],
            (640, 256),
        )
    )
    grad_mixed = order.step("attend.back", narrow(product_t(branch1, w_self)))
    grad_qkv = jnp.concatenate(
        attend_back_pair(
            key_bias, (qkv, 0), (qkv, 4), (qkv, 8), grad_mixed, mixed, levels, True
        ),
        1,
    )
    part0 = product_t(order.step("part0", grad_qkv), w_qkv)
    sums = jnp.stack(
        [
            jnp.sum(part0 * unit0, 0),
            jnp.sum(part1 * unit1, 0),
            jnp.sum(part2 * unit2, 0),
            jnp.sum(part0, 0),
            jnp.sum(part1, 0),
            jnp.sum(part2, 0),
            0.5 * jnp.sum(wide(grad_encoded), 0),
            jnp.zeros((D,), jnp.float32),
        ]
    )
    sums = jnp.pad(narrow(sums).reshape(PARTS, 2, D), ((0, 0), (0, 14), (0, 0)))
    late_blocks = group_blocks(
        place,
        [
            (order.step("late", normed0), grad_qkv, [(0, 128, 128, 0), (128, 128, 272, 0)]),
            (mixed, branch1, [(0, 128, 0, 0)]),
        ],
        (416, 384),
        sums,
    )
    order.note("blocks", late_blocks[0])
    norm0_mine, norm0_other = split_rows(order.behind("<scale", part0))
    grad_norm0 = norm0_mine + wide(partner(narrow(norm0_other)))
    unit0_mine, scale0_mine = normalise(wide(order.behind("<scale", frames_mine)))
    after_self_mine, _ = split_rows(order.behind("<scale", grad_after_self))
    grad_inputs = after_self_mine + normal_back(unit0_mine, scale0_mine, gains[0], grad_norm0)
    moved = stage_exchange(
        order.behind("<moved", jnp.concatenate([narrow(grad_inputs), text_result], 1))
    )
    order.note("moved", moved)
    result_mine, result_other = split_rows(product(order.behind("<result", hidden), w_out))
    base_mine, _ = split_rows(after_cross)
    result = stage_exchange(narrow(base_mine + result_mine + wide(partner(narrow(result_other)))))
    order.note("result", result)
    late_sums = Reduction(order, "late", late_blocks)
    longs, shorts = moved[: STAGES // 2], moved[STAGES // 2 :]
    words_at = slice(rows, rows + own_words)

    (feed_out_grad,) = finish(
        place, out_sums.block(), [(feed_out.shape, [(..., 256, lambda part: part * 256)])]
    )

    def interleaved(width):
        return [
            ((side,), width, lambda part, side=side: (2 * part + side) * width)
            for side in range(2)
        ]

    (feed_in_grad,) = finish(
        place, own_rows(in_sums.block()), [(feed_in.shape, interleaved(512))]
    )
    cross_block, shard = cross_sums.block(), D // 8
    sides = own_rows(
        cross_block[shard:].reshape(2, 2, shard, 256).transpose(1, 0, 2, 3).reshape(4 * shard, 256)
    )
    cross_block = jnp.concatenate([cross_block[:shard], sides.reshape(4 * shard, 256)], 0)

    def rows_at(first, count=shard, lanes=slice(None)):
        return (slice(first, first + count), lanes)

    cross_out_grad, cross_query_grad, text_proj_grad, cross_keyval_grad = finish(
        place,
        cross_block,
        [
            (cross_out.shape, [(rows_at(0), 256, lambda part: part * 256)]),
            (
                cross_query.shape,
                [
                    (
                        rows_at((1 + 2 * side) * shard, shard, slice(0, 128)),
                        128,
                        lambda part, side=side: (2 * part + side) * 128,
                    )
                    for side in range(2)
                ],
            ),
            (
                text_proj.shape,
                [
                    (
                        rows_at((1 + 2 * side) * shard, text_rows, slice(128, 256)),
                        128,
                        lambda part, side=side: side * half + part * 128,
                    )
                    for side in range(2)
                ],
            ),
            (
                cross_keyval.shape,
                [
                    (
                        rows_at((2 + 2 * side) * shard, shard, slice(128 * j, 128 * j + 128)),
                        128,
                        lambda part, side=side, j=j: (2 * (2 * part + j) + side) * 128,
                    )
                    for side in range(2)
                    for j in range(2)
                ],
            ),
        ],
    )
    late_block = late_sums.block()
    sides = own_rows(late_block[shard:]).reshape(2 * (shard + 16), 384)
    self_out_grad, qkv_grad, sums = finish(
        place,
        jnp.concatenate([late_block[:shard], sides], 0),
        [
            (self_out.shape, [(rows_at(0, shard, slice(0, 256)), 256, lambda part: part * 256)]),
            (
                qkv_weight.shape,
                [
                    (
                        rows_at(
                            shard + side * (shard + 16), shard, slice(128 * j, 128 * j + 128)
                        ),
                        128,
                        lambda part, side=side, j=j: (2 * (3 * part + j) + side) * 128,
                    )
                    for side in range(2)
                    for j in range(3)
                ],
            ),
        ],
        (2 * shard, 3 * shard + 16),
    )
    sums = sums[:, :2].reshape(8, shard)
    return (
        result[: STAGES // 2],
        result[STAGES // 2 :, :short_rows],
        wide(longs[:, :rows]),
        wide(shorts[:, :short_rows]),
        wide(longs[:, words_at, :ENC]),
        wide(shorts[:, words_at, :ENC]),
        qkv_grad,
        self_out_grad,
        cross_query_grad,
        cross_keyval_grad,
        cross_out_grad,
        text_proj_grad,
        sums[6],
        feed_in_grad,
        feed_out_grad,
        sums[0:3],
        sums[3:6],
    )


def solution(mesh):
    return jax.shard_map(
        on_item_device if fits_item_plan(mesh) else on_device,
        mesh=mesh,
        in_specs=(
            P("dp", "seq", None),
            P("dp", "seq", None),
            P("dp", None, None),
            P("dp", None, None),
            P("dp"),
            P("dp"),
            P(None, "dp"),
            P("seq", None),
            P("seq", None),
            P("seq", None),
            P("seq", None),
            P("seq", None),
            P("seq", None),
            P("seq"),
            P("seq", None),
            P("seq", None),
            P(None, "seq"),
            P(None, "seq"),
            P("dp", "seq", None),
            P("dp", "seq", None),
        ),
        out_specs=(
            P("dp", "seq", None),
            P("dp", "seq", None),
            P("dp", "seq", None),
            P("dp", "seq", None),
            P("dp", "seq", None),
            P("dp", "seq", None),
            P("seq", None),
            P("seq", None),
            P("seq", None),
            P("seq", None),
            P("seq", None),
            P("seq", None),
            P("seq"),
            P("seq", None),
            P("seq", None),
            P(None, "seq"),
            P(None, "seq"),
        ),
        check_vma=False,
    )
```
